32 devices in a mesh: row: 8 (over y, x, core), col: 4 (over z).
Axes of the slice: x: 2, y: 2, z: 4, core: 2. Of those that a mesh axis runs over, the one named last changes fastest.
Arguments:
- points: float32 [8, 4096], P(None, ('row', 'col')), may hold values from -1.8 to 1.8
- inverse_scale: float32 [8], replicated, may hold values from 0.5 to 1
- targets: float32 [16, 4096], P(None, ('row', 'col')), may hold values from -3.5 to 5.5
- noise_var: float32 [16], replicated, may hold values from 0.5 to 2
Outputs:
- solution: float32 [16, 4096], P(None, ('row', 'col'))
- residual: float32 [16, 4096], P(None, ('row', 'col'))
The draws below stay inside these ranges and needn't reach their ends.
All inputs are finite; a program needn't handle non-finite values.
Results may differ from the reference program's by a relative error of at most 0.0015.
Values sent between devices are 32-bit elements; how exact they have to be, the bound alone decides.
A program may use at most 64 MiB of HBM per device.

```python
import math
import jax
import jax.numpy as jnp
from jax import lax

NFEAT = 8
NRHS = 16
ITERS = 2
NPTS = 4096


def draw_targets(key, part):
    key = jax.random.fold_in(key, 7)
    offset_key, noise_key = jax.random.split(key)
    offset = jax.random.uniform(offset_key, (NRHS, 1), jnp.float32, 0.5, 1.5)
    noise = jax.random.truncated_normal(noise_key, -4.0, 4.0, (NRHS, NPTS), jnp.float32)
    return (offset + noise).astype(jnp.float32)


def block_levels(key, dims, pieces, low, high):
    gain, own = 1.0, jax.random.fold_in(key, 6)
    for dim, shards_of in pieces:
        steps = jnp.exp(jax.random.uniform(jax.random.fold_in(own, dim), (shards_of,), jnp.float32, low / len(pieces), high / len(pieces)))
        gain = gain * jnp.repeat(steps, dims[dim] // shards_of).reshape([-1 if axis == dim else 1 for axis in range(len(dims))])
    return gain


def setup_inputs(seed: int = 0) -> dict:
    seeds = jax.random.split(jax.random.key(seed), 5)
    return {
        "points": jnp.clip(jax.random.uniform(seeds[0], (NFEAT, NPTS), jnp.float32, -1.8, 1.8) * block_levels(seeds[0], (NFEAT, NPTS), ((1, 32),), -0.4, 0.0), -1.8, 1.8),
        "inverse_scale": jnp.clip(jnp.exp(jax.random.uniform(seeds[1], (NFEAT,), jnp.float32, math.log(0.5), math.log(1.0))), 0.5, 1.0),
        "targets": draw_targets(jax.random.fold_in(seeds[4], 71), 0),
        "noise_var": jnp.clip(jnp.exp(jax.random.uniform(seeds[3], (NRHS,), jnp.float32, math.log(0.5), math.log(2.0))), 0.5, 2.0),
    }


exact_mode = lax.Precision.HIGHEST


def kernel_apply(scaled, vector):
    column_count = scaled.shape[1]
    block_cols = math.gcd(column_count, 1024)
    block_count = column_count // block_cols
    half_norms = 0.5 * jnp.sum(scaled * scaled, axis=0)

    def advance(accumulated, block_index):
        offset = (block_index * block_cols).astype(jnp.int32)
        col_z = lax.dynamic_slice_in_dim(scaled, offset, block_cols, 1)
        col_v = lax.dynamic_slice_in_dim(vector, offset, block_cols, 1)
        col_half = 0.5 * jnp.sum(col_z * col_z, axis=0)
        inner_products = jnp.einsum("fb,fr->br", col_z, scaled, precision=exact_mode)
        kernel = jnp.exp(inner_products - col_half[:, None] - half_norms[None, :])
        return accumulated + jnp.dot(col_v, kernel, precision=exact_mode, preferred_element_type=jnp.float32), None

    initial = jnp.zeros(vector.shape, jnp.float32)
    accumulated, unused = lax.scan(advance, initial, jnp.arange(block_count, dtype=jnp.int32))
    return accumulated


def reference(points, inverse_scale, targets, noise_var):
    scaled = points * inverse_scale[:, None]
    solution = jnp.zeros_like(targets)
    residual = targets
    direction = targets
    norm_now = jnp.sum(residual * residual, axis=1)
    for turn in range(ITERS):
        image = kernel_apply(scaled, direction) + noise_var[:, None] * direction
        step_size = norm_now / jnp.sum(direction * image, axis=1)
        solution = solution + step_size[:, None] * direction
        residual = residual - step_size[:, None] * image
        norm_next = jnp.sum(residual * residual, axis=1)
        direction = residual + (norm_next / norm_now)[:, None] * direction
        norm_now = norm_next
    return solution, residual
```

```python
import functools
import math
import jax
import jax.numpy as jnp
from jax import lax
from jax.experimental import pallas as pl
from jax.experimental.pallas import tpu as pltpu
from jax.sharding import PartitionSpec as P

MESH = pl.DeviceIdType.MESH
ROOT = math.sqrt(1.0 / math.log(2.0))


def loop(low, high, body):
    if high - low <= 32:
        for k in range(low, high):
            body(k)
    else:

        def step(k, carry):
            body(k)
            return carry

        lax.fori_loop(low, high, step, 0)


def three(x):
    high = x.astype(jnp.bfloat16).astype(jnp.float32)
    rest = x - high
    middle = rest.astype(jnp.bfloat16).astype(jnp.float32)
    return high, middle, rest - middle


def two(x):
    high = x.astype(jnp.bfloat16)
    low = (x - high.astype(jnp.float32)).astype(jnp.bfloat16)
    return jnp.concatenate([high, low], axis=0)


def factors(z, left):
    z = z * ROOT
    half = 0.5 * jnp.sum(z * z, axis=0, keepdims=True)
    h, m, l = three(z)
    a, b, c = three(-half)
    row = lax.broadcasted_iota(jnp.int32, z.shape, 0)
    norms = jnp.where(row == 0, a, jnp.where(row == 1, b, jnp.where(row == 2, c, 0.0)))
    ones = jnp.ones_like(z)
    parts = [h, h, m, h, l, m, norms, ones] if left else [h, m, h, l, h, m, ones, norms]
    return jnp.concatenate(parts, axis=0).astype(jnp.bfloat16)


def column(ref, count, lanes):
    row = lax.broadcasted_iota(jnp.int32, (count, lanes), 0)
    out = jnp.zeros((count, lanes), jnp.float32)
    for k in range(count):
        out = jnp.where(row == k, ref[k], out)
    return out


def lane_sums(parts):
    used = sum(p.shape[0] for p in parts)
    parts = parts + [jnp.zeros((128 - used, 128), jnp.float32)]
    return jnp.sum(jnp.concatenate(parts, axis=0).T, axis=0, keepdims=True)


def to_column(row):
    return jnp.broadcast_to(row, (128, 128)).T


def kernel(
    nr, nc, feats, rhs, lanes,
    points_ref, scale_ref, targets_ref, noise_ref,
    solution_ref, residual_ref,
    raw, plane, line, part, wplane, wline, part2, tiny, tiny2, khi, klo,
    load_sem, send_sem, recv_p, recv_l, recv_part, recv_wp, recv_wl, recv_part2, recv_tiny, recv_tiny2,
):
    r, c = lax.axis_index("row"), lax.axis_index("col")
    every = nr * nc

    def at(kr, kc):
        return (lax.rem(r + kr, nr), lax.rem(c + kc, nc))

    load_points = pltpu.make_async_copy(points_ref, raw, load_sem.at[0])
    load_targets = pltpu.make_async_copy(targets_ref, plane.at[0, pl.ds(feats, rhs)], load_sem.at[1])
    load_points.start()
    load_targets.start()
    barrier = pltpu.get_barrier_semaphore()
    loop(1, nr, lambda k: pl.semaphore_signal(barrier, inc=1, device_id=at(k, 0), device_id_type=MESH))
    loop(1, nc, lambda k: pl.semaphore_signal(barrier, inc=1, device_id=at(0, k), device_id_type=MESH))
    scale = column(scale_ref, feats, lanes)
    noise = column(noise_ref, rhs, lanes)
    load_points.wait()
    plane[0, 0:feats, :] = raw[...] * scale
    load_targets.wait()
    line[0] = plane[0]
    pl.semaphore_wait(barrier, nr + nc - 2)

    def send(src, dst, slot, recv, device):
        return pltpu.make_async_remote_copy(
            src_ref=src, dst_ref=dst, send_sem=send_sem.at[slot], recv_sem=recv,
            device_id=device, device_id_type=MESH,
        )

    base = [0]

    def group(low, high, make):
        start = base[0]
        base[0] += high - low

        def copy(k):
            return make(k, start + k - low)

        return low, high, copy

    def begin(g):
        loop(g[0], g[1], lambda k: g[2](k).start())

    def arrived(g):
        loop(g[0], g[1], lambda k: g[2](k).wait_recv())

    def sent(g):
        loop(g[0], g[1], lambda k: g[2](k).wait_send())

    to_line = group(1, nc, lambda k, s: send(line.at[0], line.at[k], s, recv_l.at[k], at(0, k)))
    to_plane = group(1, nr, lambda k, s: send(plane.at[0], plane.at[k], s, recv_p.at[k], at(k, 0)))
    begin(to_line)
    begin(to_plane)

    arrived(to_line)
    right = factors(jnp.concatenate([line[k, 0:feats, :] for k in range(nc)], axis=1), False)
    arrived(to_plane)

    pair = 2 if nr % 2 == 0 else 1
    depth = pair * lanes

    def first(step, total):
        z = jnp.concatenate([plane[step * pair + k, 0:feats, :] for k in range(pair)], axis=1)
        v = jnp.concatenate([plane[step * pair + k, feats : feats + rhs, :] for k in range(pair)], axis=1)
        power = lax.dot_general(
            factors(z, True), right, (((0,), (0,)), ((), ())), preferred_element_type=jnp.float32
        )
        tile = jnp.exp2(power)
        high = tile.astype(jnp.bfloat16)
        low = (tile - high.astype(jnp.float32)).astype(jnp.bfloat16)
        khi[step] = high
        klo[step] = low
        v = two(v)
        both = jnp.dot(v, high, preferred_element_type=jnp.float32)
        return total + both[:rhs] + both[rhs:] + jnp.dot(v, low, preferred_element_type=jnp.float32)[:rhs]

    def steps(body):
        total = jnp.zeros((rhs, nc * lanes), jnp.float32)
        if nr // pair <= 8:
            for step in range(nr // pair):
                total = body(step, total)
            return total
        return lax.fori_loop(0, nr // pair, body, total)

    partial = steps(first)
    for k in range(nc):
        part[nc + k] = partial[:, k * lanes : (k + 1) * lanes]
    give = group(1, nc, lambda k, s: send(part.at[nc + k], part.at[k], s, recv_part.at[k], at(0, nc - k)))
    begin(give)
    target = plane[0, feats : feats + rhs, :]
    image = part[nc] + noise * target
    arrived(give)
    for k in range(1, nc):
        image = image + part[k]

    wplane[0] = image
    wline[0] = image
    w_line = group(1, nc, lambda k, s: send(wline.at[0], wline.at[k], s, recv_wl.at[k], at(0, k)))
    w_plane = group(1, nr, lambda k, s: send(wplane.at[0], wplane.at[k], s, recv_wp.at[k], at(k, 0)))
    begin(w_line)
    begin(w_plane)
    tiny[0] = lane_sums([target * target, target * image, image * image])

    def spread(ref, recv):
        def make(k, s):
            return send(ref.at[0], ref.at[k], s, recv.at[k], at(k // nc, lax.rem(k, nc)))

        return group(1, every, make)

    scalars = spread(tiny, recv_tiny)
    begin(scalars)
    arrived(w_line)
    arrived(w_plane)
    arrived(scalars)

    sums = to_column(jnp.sum(tiny[...], axis=0))
    tt, tw, ww = sums[:rhs], sums[rhs : 2 * rhs], sums[2 * rhs : 3 * rhs]
    alpha = tt / tw
    beta = alpha * alpha * ww / tt - 1.0

    def direct(t, w):
        return (t - alpha * w) + beta * t

    def second(step, total):
        v = two(jnp.concatenate(
            [direct(plane[step * pair + k, feats : feats + rhs, :], wplane[step * pair + k]) for k in range(pair)],
            axis=1,
        ))
        both = jnp.dot(v, khi[step], preferred_element_type=jnp.float32)
        return total + both[:rhs] + both[rhs:] + jnp.dot(v, klo[step], preferred_element_type=jnp.float32)[:rhs]

    partial = steps(second)
    for k in range(nc):
        part2[nc + k] = partial[:, k * lanes : (k + 1) * lanes]
    give2 = group(1, nc, lambda k, s: send(part2.at[nc + k], part2.at[k], s, recv_part2.at[k], at(0, nc - k)))
    begin(give2)
    residual = target - alpha * image
    direction = direct(target, image)
    curved = noise * direction * direction
    for k in range(nc):
        curved = curved + direct(line[k, feats : feats + rhs, :], wline[k]) * partial[:, k * lanes : (k + 1) * lanes]
    tiny2[0] = lane_sums([curved, residual * residual])
    scalars2 = spread(tiny2, recv_tiny2)
    begin(scalars2)
    image2 = part2[nc] + noise * direction
    arrived(give2)
    for k in range(1, nc):
        image2 = image2 + part2[k]
    arrived(scalars2)
    sums = to_column(jnp.sum(tiny2[...], axis=0))
    alpha2 = sums[rhs : 2 * rhs] / sums[:rhs]
    solution_ref[...] = alpha * target + alpha2 * direction
    residual_ref[...] = residual - alpha2 * image2
    for g in (to_line, to_plane, give, w_line, w_plane, scalars, give2, scalars2):
        sent(g)


def solution(mesh):
    nr, nc = mesh.shape["row"], mesh.shape["col"]

    def on_device(points, inverse_scale, targets, noise_var):
        feats, lanes = points.shape
        rhs = targets.shape[0]
        pair = 2 if nr % 2 == 0 else 1
        every = nr * nc
        f32 = jnp.float32
        block = jax.ShapeDtypeStruct((rhs, lanes), f32)
        dma = pltpu.SemaphoreType.DMA
        sends = 4 * (nc - 1) + 2 * (nr - 1) + 2 * (every - 1)
        return pl.pallas_call(
            functools.partial(kernel, nr, nc, feats, rhs, lanes),
            out_shape=(block, block),
            in_specs=[
                pl.BlockSpec(memory_space=pl.ANY),
                pl.BlockSpec(memory_space=pltpu.SMEM),
                pl.BlockSpec(memory_space=pl.ANY),
                pl.BlockSpec(memory_space=pltpu.SMEM),
            ],
            out_specs=(pl.BlockSpec(memory_space=pltpu.VMEM),) * 2,
            scratch_shapes=[
                pltpu.VMEM((feats, lanes), f32),
                pltpu.VMEM((nr, feats + rhs, lanes), f32),
                pltpu.VMEM((nc, feats + rhs, lanes), f32),
                pltpu.VMEM((2 * nc, rhs, lanes), f32),
                pltpu.VMEM((nr, rhs, lanes), f32),
                pltpu.VMEM((nc, rhs, lanes), f32),
                pltpu.VMEM((2 * nc, rhs, lanes), f32),
                pltpu.VMEM((every, 1, lanes), f32),
                pltpu.VMEM((every, 1, lanes), f32),
                pltpu.VMEM((nr // pair, pair * lanes, nc * lanes), jnp.bfloat16),
                pltpu.VMEM((nr // pair, pair * lanes, nc * lanes), jnp.bfloat16),
                dma((2,)),
                dma((sends,)),
                dma((nr,)),
                dma((nc,)),
                dma((nc,)),
                dma((nr,)),
                dma((nc,)),
                dma((nc,)),
                dma((every,)),
                dma((every,)),
            ],
            compiler_params=pltpu.CompilerParams(
                collective_id=0, has_side_effects=True, vmem_limit_bytes=56 * 1024 * 1024
            ),
        )(points, inverse_scale, targets, noise_var)

    spec = P(None, ("row", "col"))
    return jax.shard_map(
        on_device, mesh=mesh, in_specs=(spec, P(), spec, P()), out_specs=(spec, spec), check_vma=False
    )
```

```python
import functools
import math
import jax
import jax.numpy as jnp
from jax import lax
from jax.experimental import pallas as pl
from jax.experimental.pallas import tpu as pltpu
from jax.sharding import PartitionSpec as P

MESH = pl.DeviceIdType.MESH
ROOT = math.sqrt(1.0 / math.log(2.0))


def loop(low, high, body):
    if high - low <= 32:
        for k in range(low, high):
            body(k)
    else:

        def step(k, carry):
            body(k)
            return carry

        lax.fori_loop(low, high, step, 0)


def three(x):
    high = x.astype(jnp.bfloat16).astype(jnp.float32)
    rest = x - high
    middle = rest.astype(jnp.bfloat16).astype(jnp.float32)
    return high, middle, rest - middle


def two(x):
    high = x.astype(jnp.bfloat16)
    low = (x - high.astype(jnp.float32)).astype(jnp.bfloat16)
    return jnp.concatenate([high, low], axis=0)


def factors(z, left):
    z = z * ROOT
    half = 0.5 * jnp.sum(z * z, axis=0, keepdims=True)
    h, m, l = three(z)
    a, b, c = three(-half)
    row = lax.broadcasted_iota(jnp.int32, z.shape, 0)
    norms = jnp.where(row == 0, a, jnp.where(row == 1, b, jnp.where(row == 2, c, 0.0)))
    ones = jnp.ones_like(z)
    parts = [h, h, m, h, l, m, norms, ones] if left else [h, m, h, l, h, m, ones, norms]
    return jnp.concatenate(parts, axis=0)


def column(ref, count, lanes):
    row = lax.broadcasted_iota(jnp.int32, (count, lanes), 0)
    out = jnp.zeros((count, lanes), jnp.float32)
    for k in range(count):
        out = jnp.where(row == k, ref[k], out)
    return out


def lane_sums(parts):
    used = sum(p.shape[0] for p in parts)
    parts = parts + [jnp.zeros((128 - used, 128), jnp.float32)]
    return jnp.sum(jnp.concatenate(parts, axis=0).T, axis=0, keepdims=True)


def to_column(row):
    return jnp.broadcast_to(row, (128, 128)).T


def kernel(
    nr, nc, feats, rhs, lanes,
    points_ref, scale_in, targets_ref, noise_in,
    solution_ref, residual_ref,
    raw, scale_ref, noise_ref, plane, line, part, wplane, wline, part2, tiny, tiny2, khi, klo,
    load_sem, send_sem, recv_sem,
):
    r, c = lax.axis_index("row"), lax.axis_index("col")
    every = nr * nc

    def at(kr, kc):
        return (lax.rem(r + kr, nr), lax.rem(c + kc, nc))

    barrier = pltpu.get_barrier_semaphore()
    loop(1, nr, lambda k: pl.semaphore_signal(barrier, inc=1, device_id=at(k, 0), device_id_type=MESH))
    loop(1, nc, lambda k: pl.semaphore_signal(barrier, inc=1, device_id=at(0, k), device_id_type=MESH))
    own = pl.ds(feats, rhs)
    loads = [
        pltpu.make_async_copy(src, dst, load_sem.at[i])
        for i, (src, dst) in enumerate([
            (points_ref, raw), (scale_in, scale_ref), (targets_ref, plane.at[0, own]),
            (targets_ref, line.at[0, own]), (noise_in, noise_ref),
        ])
    ]
    for load in loads:
        load.start()
    loads[0].wait()
    loads[1].wait()
    scaled = raw[...] * column(scale_ref, feats, lanes)
    plane[0, 0:feats, :] = scaled
    line[0, 0:feats, :] = scaled
    for load in loads[2:]:
        load.wait()
    pl.semaphore_wait(barrier, nr + nc - 2)

    class Group:
        count = 0

        def __init__(self, ref, last, peer, src=lambda k: 0):
            self.ref, self.last, self.peer, self.src = ref, last, peer, src
            self.sem = Group.count
            Group.count += 1

        def start(self, low=1, high=None):
            def one(k):
                pltpu.make_async_remote_copy(
                    src_ref=self.ref.at[self.src(k)], dst_ref=self.ref.at[k],
                    send_sem=send_sem.at[self.sem], recv_sem=recv_sem.at[self.sem],
                    device_id=self.peer(k), device_id_type=MESH,
                ).start()

            loop(low, self.last if high is None else high, one)

        def wait(self, sem):
            slots = self.ref.at[pl.ds(1, self.last - 1)]
            pltpu.make_async_copy(slots, slots, sem.at[self.sem]).wait()

        def arrived(self):
            self.wait(recv_sem)

        def sent(self):
            self.wait(send_sem)

    along_col = lambda k: at(0, k)
    along_row = lambda k: at(k, 0)
    back_col = lambda k: at(0, nc - k)
    anywhere = lambda k: at(k // nc, lax.rem(k, nc))
    to_line = Group(line, nc, along_col)
    to_plane = Group(plane, nr, along_row)
    give = Group(part, nc, back_col, lambda k: nc + k)
    w_line = Group(wline, nc, along_col)
    w_plane = Group(wplane, nr, along_row)
    scalars = Group(tiny, every, anywhere)
    give2 = Group(part2, nc, back_col, lambda k: nc + k)
    scalars2 = Group(tiny2, every, anywhere)

    to_line.start()
    to_plane.start()

    pair = 2 if nr % 2 == 0 else 1
    steps = nr // pair
    wide = 2 if nc % 2 == 0 else 1
    order = list(range(1, nc)) + [0]
    order = [order[i : i + wide] for i in range(0, nc, wide)]
    few = steps <= 8

    def cached(make):
        held = {}

        def get(step):
            if not few:
                return make(step)
            if step not in held:
                held[step] = make(step)
            return held[step]

        return get

    def total(body):
        out = jnp.zeros((rhs, wide * lanes), jnp.float32)
        if few:
            for step in range(steps):
                out = body(step, out)
            return out
        return lax.fori_loop(0, steps, body, out)

    def apply(v, high, low):
        both = jnp.dot(v, high, preferred_element_type=jnp.float32)
        return both[:rhs] + both[rhs:] + jnp.dot(v, low, preferred_element_type=jnp.float32)[:rhs]

    def hand_out(columns, partial, ref, group):
        for i, k in enumerate(columns):
            ref[nc + k] = partial[:, i * lanes : (i + 1) * lanes]
            if k:
                group.start(k, k + 1)

    def across(read):
        return lambda step: jnp.concatenate([read(step * pair + k) for k in range(pair)], axis=1)

    z_of = across(lambda k: plane[k, 0:feats, :])
    t_of = across(lambda k: plane[k, feats : feats + rhs, :])
    left = cached(lambda step: factors(z_of(step), True).T.astype(jnp.bfloat16))
    first_v = cached(lambda step: two(t_of(step)))

    to_line.arrived()
    rights = [
        factors(jnp.concatenate([line[k, 0:feats, :] for k in columns], axis=1), False).astype(jnp.bfloat16)
        for columns in order
    ]
    to_plane.arrived()

    for i, columns in enumerate(order):

        def first(step, out):
            tile = jnp.exp2(jnp.dot(left(step), rights[i], preferred_element_type=jnp.float32))
            high = tile.astype(jnp.bfloat16)
            low = (tile - high.astype(jnp.float32)).astype(jnp.bfloat16)
            khi[i, step] = high
            klo[i, step] = low
            return out + apply(first_v(step), high, low)

        hand_out(columns, total(first), part, give)

    noise = column(noise_ref, rhs, lanes)
    target = plane[0, feats : feats + rhs, :]
    image = part[nc] + noise * target
    give.arrived()
    for k in range(1, nc):
        image = image + part[k]

    wplane[0] = image
    wline[0] = image
    w_plane.start()
    w_line.start()
    tiny[0] = lane_sums([target * target, target * image, image * image])
    scalars.start()
    w_line.arrived()
    w_plane.arrived()
    scalars.arrived()

    sums = to_column(jnp.sum(tiny[...], axis=0))
    tt, tw, ww = sums[:rhs], sums[rhs : 2 * rhs], sums[2 * rhs : 3 * rhs]
    alpha = tt / tw
    beta = alpha * alpha * ww / tt - 1.0

    def direct(t, w):
        return (t - alpha * w) + beta * t

    d_of = across(lambda k: direct(plane[k, feats : feats + rhs, :], wplane[k]))
    second_v = cached(lambda step: two(d_of(step)))
    residual = target - alpha * image
    direction = direct(target, image)
    curved = noise * direction * direction
    for i, columns in enumerate(order):
        partial = total(lambda step, out: out + apply(second_v(step), khi[i, step], klo[i, step]))
        hand_out(columns, partial, part2, give2)
        for k in columns:
            curved = curved + direct(line[k, feats : feats + rhs, :], wline[k]) * part2[nc + k]
    tiny2[0] = lane_sums([curved, residual * residual])
    scalars2.start()
    image2 = part2[nc] + noise * direction
    give2.arrived()
    for k in range(1, nc):
        image2 = image2 + part2[k]
    scalars2.arrived()
    sums = to_column(jnp.sum(tiny2[...], axis=0))
    alpha2 = sums[rhs : 2 * rhs] / sums[:rhs]
    solution_ref[...] = alpha * target + alpha2 * direction
    residual_ref[...] = residual - alpha2 * image2
    for g in (to_line, to_plane, give, w_line, w_plane, scalars, give2, scalars2):
        g.sent()


def solution(mesh):
    nr, nc = mesh.shape["row"], mesh.shape["col"]

    def on_device(points, inverse_scale, targets, noise_var):
        feats, lanes = points.shape
        rhs = targets.shape[0]
        pair = 2 if nr % 2 == 0 else 1
        wide = 2 if nc % 2 == 0 else 1
        every = nr * nc
        f32 = jnp.float32
        block = jax.ShapeDtypeStruct((rhs, lanes), f32)
        dma = pltpu.SemaphoreType.DMA
        tiles = (nc // wide, nr // pair, pair * lanes, wide * lanes)
        anywhere = pl.BlockSpec(memory_space=pl.ANY)
        return pl.pallas_call(
            functools.partial(kernel, nr, nc, feats, rhs, lanes),
            out_shape=(pltpu.VMEM((rhs, lanes), f32),) * 2,
            in_specs=[anywhere] * 4,
            out_specs=(pl.BlockSpec(memory_space=pltpu.VMEM),) * 2,
            scratch_shapes=[
                pltpu.VMEM((feats, lanes), f32),
                pltpu.SMEM((feats,), f32),
                pltpu.SMEM((rhs,), f32),
                pltpu.VMEM((nr, feats + rhs, lanes), f32),
                pltpu.VMEM((nc, feats + rhs, lanes), f32),
                pltpu.VMEM((2 * nc, rhs, lanes), f32),
                pltpu.VMEM((nr, rhs, lanes), f32),
                pltpu.VMEM((nc, rhs, lanes), f32),
                pltpu.VMEM((2 * nc, rhs, lanes), f32),
                pltpu.VMEM((every, 1, lanes), f32),
                pltpu.VMEM((every, 1, lanes), f32),
                pltpu.VMEM(tiles, jnp.bfloat16),
                pltpu.VMEM(tiles, jnp.bfloat16),
                dma((5,)),
                dma((8,)),
                dma((8,)),
            ],
            compiler_params=pltpu.CompilerParams(
                collective_id=0, has_side_effects=True, vmem_limit_bytes=56 * 1024 * 1024
            ),
        )(points, inverse_scale, targets, noise_var)

    spec = P(None, ("row", "col"))
    return jax.shard_map(
        on_device, mesh=mesh, in_specs=(spec, P(), spec, P()), out_specs=(spec, spec), check_vma=False
    )
```

```python
import functools
import math
import jax
import jax.numpy as jnp
from jax import lax
from jax.experimental import pallas as pl
from jax.experimental.pallas import tpu as pltpu
from jax.sharding import PartitionSpec as P

MESH = pl.DeviceIdType.MESH
ROOT = math.sqrt(1.0 / math.log(2.0))


def loop(low, high, body):
    if high - low <= 32:
        for k in range(low, high):
            body(k)
    else:

        def step(k, carry):
            body(k)
            return carry

        lax.fori_loop(low, high, step, 0)


def three(x):
    high = x.astype(jnp.bfloat16).astype(jnp.float32)
    rest = x - high
    middle = rest.astype(jnp.bfloat16).astype(jnp.float32)
    return high, middle, rest - middle


def two(x):
    high = x.astype(jnp.bfloat16)
    low = (x - high.astype(jnp.float32)).astype(jnp.bfloat16)
    return jnp.concatenate([high, low], axis=0)


def factors(z, left):
    z = z * ROOT
    half = 0.5 * jnp.sum(z * z, axis=0, keepdims=True)
    h, m, l = three(z)
    a, b, c = three(-half)
    row = lax.broadcasted_iota(jnp.int32, z.shape, 0)
    norms = jnp.where(row == 0, a, jnp.where(row == 1, b, jnp.where(row == 2, c, 0.0)))
    ones = jnp.ones_like(z)
    parts = [h, h, m, h, l, m, norms, ones] if left else [h, m, h, l, h, m, ones, norms]
    return jnp.concatenate(parts, axis=0)


def column(ref, count, lanes):
    row = lax.broadcasted_iota(jnp.int32, (count, lanes), 0)
    out = jnp.zeros((count, lanes), jnp.float32)
    for k in range(count):
        out = jnp.where(row == k, ref[k], out)
    return out


def lane_sums(parts):
    used = sum(p.shape[0] for p in parts)
    parts = parts + [jnp.zeros((128 - used, 128), jnp.float32)]
    return jnp.sum(jnp.concatenate(parts, axis=0).T, axis=0, keepdims=True)


def to_column(row):
    return jnp.broadcast_to(row, (128, 128)).T


def kernel(
    nr, nc, feats, rhs, lanes,
    points_ref, scale_in, targets_ref, noise_in,
    solution_ref, residual_ref,
    raw, scale_ref, noise_ref, plane, line, part, wplane, wline, part2, tiny, tiny2, khi, klo,
    load_sem, send_sem, recv_sem,
):
    r, c = lax.axis_index("row"), lax.axis_index("col")
    every = nr * nc

    def turn(position, k, count):
        moved = position + k
        return jnp.where(moved >= count, moved - count, moved)

    rows = [r] + [turn(r, k, nr) for k in range(1, nr)] if every <= 32 else None
    cols = [c] + [turn(c, k, nc) for k in range(1, nc)] if every <= 32 else None

    def at(kr, kc):
        if rows is not None:
            return (rows[kr], cols[kc])
        return (turn(r, kr, nr), turn(c, kc, nc))

    barrier = pltpu.get_barrier_semaphore()
    loop(1, nr, lambda k: pl.semaphore_signal(barrier, inc=1, device_id=at(k, 0), device_id_type=MESH))
    loop(1, nc, lambda k: pl.semaphore_signal(barrier, inc=1, device_id=at(0, k), device_id_type=MESH))
    own = pl.ds(feats, rhs)
    loads = [
        pltpu.make_async_copy(src, dst, load_sem.at[i])
        for i, (src, dst) in enumerate([
            (points_ref, raw), (scale_in, scale_ref), (targets_ref, plane.at[0, own]),
            (targets_ref, line.at[0, own]), (noise_in, noise_ref),
        ])
    ]
    for load in loads:
        load.start()
    loads[0].wait()
    loads[1].wait()
    scaled = raw[...] * column(scale_ref, feats, lanes)
    plane[0, 0:feats, :] = scaled
    line[0, 0:feats, :] = scaled
    for load in loads[2:]:
        load.wait()
    pl.semaphore_wait(barrier, nr + nc - 2)

    class Group:
        count = 0

        def __init__(self, ref, last, peer, src=lambda k: 0):
            self.ref, self.last, self.peer, self.src = ref, last, peer, src
            self.sem = Group.count
            Group.count += 1

        def start(self, low=1, high=None):
            def one(k):
                pltpu.make_async_remote_copy(
                    src_ref=self.ref.at[self.src(k)], dst_ref=self.ref.at[k],
                    send_sem=send_sem.at[self.sem], recv_sem=recv_sem.at[self.sem],
                    device_id=self.peer(k), device_id_type=MESH,
                ).start()

            loop(low, self.last if high is None else high, one)

        def wait(self, sem):
            slots = self.ref.at[pl.ds(1, self.last - 1)]
            pltpu.make_async_copy(slots, slots, sem.at[self.sem]).wait()

        def arrived(self):
            self.wait(recv_sem)

        def sent(self):
            self.wait(send_sem)

    along_col = lambda k: at(0, k)
    along_row = lambda k: at(k, 0)
    back_col = lambda k: at(0, nc - k)
    anywhere = lambda k: at(k // nc, k % nc)
    to_line = Group(line, nc, along_col)
    to_plane = Group(plane, nr, along_row)
    give = Group(part, nc, back_col, lambda k: nc + k)
    w_line = Group(wline, nc, along_col)
    w_plane = Group(wplane, nr, along_row)
    scalars = Group(tiny, every, anywhere)
    give2 = Group(part2, nc, back_col, lambda k: nc + k)
    scalars2 = Group(tiny2, every, anywhere)

    to_line.start()
    to_plane.start()

    pair = 2 if nr % 2 == 0 else 1
    steps = nr // pair
    wide = 2 if nc % 2 == 0 else 1
    order = list(range(1, nc)) + [0]
    order = [order[i : i + wide] for i in range(0, nc, wide)]
    few = steps <= 8

    def cached(make):
        held = {}

        def get(step):
            if not few:
                return make(step)
            if step not in held:
                held[step] = make(step)
            return held[step]

        return get

    def total(body):
        out = jnp.zeros((rhs, wide * lanes), jnp.float32)
        if few:
            for step in range(steps):
                out = body(step, out)
            return out
        return lax.fori_loop(0, steps, body, out)

    def apply(v, high, low):
        both = jnp.dot(v, high, preferred_element_type=jnp.float32)
        return both[:rhs] + both[rhs:] + jnp.dot(v, low, preferred_element_type=jnp.float32)[:rhs]

    def hand_out(columns, partial, ref, group):
        for i, k in enumerate(columns):
            ref[nc + k] = partial[:, i * lanes : (i + 1) * lanes]
            if k:
                group.start(k, k + 1)

    def across(read):
        return lambda step: jnp.concatenate([read(step * pair + k) for k in range(pair)], axis=1)

    z_of = across(lambda k: plane[k, 0:feats, :])
    t_of = across(lambda k: plane[k, feats : feats + rhs, :])
    left = cached(lambda step: factors(z_of(step), True).T.astype(jnp.bfloat16))
    first_v = cached(lambda step: two(t_of(step)))

    to_line.arrived()
    rights = [
        factors(jnp.concatenate([line[k, 0:feats, :] for k in columns], axis=1), False).astype(jnp.bfloat16)
        for columns in order
    ]
    to_plane.arrived()

    for i, columns in enumerate(order):

        def first(step, out):
            tile = jnp.exp2(jnp.dot(left(step), rights[i], preferred_element_type=jnp.float32))
            high = tile.astype(jnp.bfloat16)
            low = (tile - high.astype(jnp.float32)).astype(jnp.bfloat16)
            khi[i, step] = high
            klo[i, step] = low
            return out + apply(first_v(step), high, low)

        hand_out(columns, total(first), part, give)

    noise = column(noise_ref, rhs, lanes)
    target = plane[0, feats : feats + rhs, :]
    image = part[nc] + noise * target
    give.arrived()
    for k in range(1, nc):
        image = image + part[k]

    wplane[0] = image
    wline[0] = image
    w_plane.start()
    tiny[0] = lane_sums([target * target, target * image, image * image])
    scalars.start()
    w_line.start()
    w_plane.arrived()
    scalars.arrived()

    sums = to_column(jnp.sum(tiny[...], axis=0))
    tt, tw, ww = sums[:rhs], sums[rhs : 2 * rhs], sums[2 * rhs : 3 * rhs]
    alpha = tt / tw
    beta = alpha * alpha * ww / tt - 1.0

    def direct(t, w):
        return (t - alpha * w) + beta * t

    d_of = across(lambda k: direct(plane[k, feats : feats + rhs, :], wplane[k]))
    second_v = cached(lambda step: two(d_of(step)))
    residual = target - alpha * image
    direction = direct(target, image)
    curved = noise * direction * direction
    for i, columns in enumerate(order):
        partial = total(lambda step, out: out + apply(second_v(step), khi[i, step], klo[i, step]))
        hand_out(columns, partial, part2, give2)
        if i == 0:
            w_line.arrived()
        for k in columns:
            curved = curved + direct(line[k, feats : feats + rhs, :], wline[k]) * part2[nc + k]
    tiny2[0] = lane_sums([curved, residual * residual])
    scalars2.start()
    image2 = part2[nc] + noise * direction
    give2.arrived()
    for k in range(1, nc):
        image2 = image2 + part2[k]
    scalars2.arrived()
    sums = to_column(jnp.sum(tiny2[...], axis=0))
    alpha2 = sums[rhs : 2 * rhs] / sums[:rhs]
    solution_ref[...] = alpha * target + alpha2 * direction
    residual_ref[...] = residual - alpha2 * image2
    for g in (to_line, to_plane, give, w_line, w_plane, scalars, give2, scalars2):
        g.sent()


def write(solution_ref, residual_ref, solution_out, residual_out, sem):
    first = pltpu.make_async_copy(solution_ref, solution_out, sem.at[0])
    second = pltpu.make_async_copy(residual_ref, residual_out, sem.at[1])
    first.start()
    second.start()
    first.wait()
    second.wait()


def solution(mesh):
    nr, nc = mesh.shape["row"], mesh.shape["col"]

    def on_device(points, inverse_scale, targets, noise_var):
        feats, lanes = points.shape
        rhs = targets.shape[0]
        pair = 2 if nr % 2 == 0 else 1
        wide = 2 if nc % 2 == 0 else 1
        every = nr * nc
        f32 = jnp.float32
        block = jax.ShapeDtypeStruct((rhs, lanes), f32)
        dma = pltpu.SemaphoreType.DMA
        tiles = (nc // wide, nr // pair, pair * lanes, wide * lanes)
        anywhere = pl.BlockSpec(memory_space=pl.ANY)
        results = pl.pallas_call(
            functools.partial(kernel, nr, nc, feats, rhs, lanes),
            out_shape=(pltpu.VMEM((rhs, lanes), f32),) * 2,
            in_specs=[anywhere] * 4,
            out_specs=(pl.BlockSpec(memory_space=pltpu.VMEM),) * 2,
            scratch_shapes=[
                pltpu.VMEM((feats, lanes), f32),
                pltpu.SMEM((feats,), f32),
                pltpu.SMEM((rhs,), f32),
                pltpu.VMEM((nr, feats + rhs, lanes), f32),
                pltpu.VMEM((nc, feats + rhs, lanes), f32),
                pltpu.VMEM((2 * nc, rhs, lanes), f32),
                pltpu.VMEM((nr, rhs, lanes), f32),
                pltpu.VMEM((nc, rhs, lanes), f32),
                pltpu.VMEM((2 * nc, rhs, lanes), f32),
                pltpu.VMEM((every, 1, lanes), f32),
                pltpu.VMEM((every, 1, lanes), f32),
                pltpu.VMEM(tiles, jnp.bfloat16),
                pltpu.VMEM(tiles, jnp.bfloat16),
                dma((5,)),
                dma((8,)),
                dma((8,)),
            ],
            compiler_params=pltpu.CompilerParams(
                collective_id=0, has_side_effects=True, vmem_limit_bytes=56 * 1024 * 1024
            ),
        )(points, inverse_scale, targets, noise_var)
        return pl.pallas_call(
            write,
            out_shape=(block, block),
            in_specs=[pl.BlockSpec(memory_space=pltpu.VMEM)] * 2,
            out_specs=(anywhere, anywhere),
            scratch_shapes=[dma((2,))],
        )(*results)

    spec = P(None, ("row", "col"))
    return jax.shard_map(
        on_device, mesh=mesh, in_specs=(spec, P(), spec, P()), out_specs=(spec, spec), check_vma=False
    )
```

```python
import functools
import math
import jax
import jax.numpy as jnp
from jax import lax
from jax.experimental import pallas as pl
from jax.experimental.pallas import tpu as pltpu
from jax.sharding import PartitionSpec as P

FEW = 8
MESH = pl.DeviceIdType.MESH
ROOT = math.sqrt(1.0 / math.log(2.0))


def loop(low, high, body):
    if high - low <= 32:
        for k in range(low, high):
            body(k)
    else:

        def step(k, carry):
            body(k)
            return carry

        lax.fori_loop(low, high, step, 0)


def three(x):
    high = x.astype(jnp.bfloat16).astype(jnp.float32)
    rest = x - high
    middle = rest.astype(jnp.bfloat16).astype(jnp.float32)
    return high, middle, rest - middle


def two(x):
    high = x.astype(jnp.bfloat16)
    low = (x - high.astype(jnp.float32)).astype(jnp.bfloat16)
    return jnp.concatenate([high, low], axis=0)


def factors(z, left):
    z = z * ROOT
    half = 0.5 * jnp.sum(z * z, axis=0, keepdims=True)
    h, m, l = three(z)
    a, b, c = three(-half)
    row = lax.broadcasted_iota(jnp.int32, z.shape, 0)
    norms = jnp.where(row == 0, a, jnp.where(row == 1, b, jnp.where(row == 2, c, 0.0)))
    ones = jnp.ones_like(z)
    parts = [h, h, m, h, l, m, norms, ones] if left else [h, m, h, l, h, m, ones, norms]
    return jnp.concatenate(parts, axis=0)


def column(ref, count, lanes):
    row = lax.broadcasted_iota(jnp.int32, (count, lanes), 0)
    out = jnp.zeros((count, lanes), jnp.float32)
    for k in range(count):
        out = jnp.where(row == k, ref[k], out)
    return out


def lane_sums(parts):
    used = sum(p.shape[0] for p in parts)
    parts = parts + [jnp.zeros((128 - used, 128), jnp.float32)]
    return jnp.sum(jnp.concatenate(parts, axis=0).T, axis=0, keepdims=True)


def to_column(row):
    return jnp.broadcast_to(row, (128, 128)).T


def kernel(
    nr, nc, feats, rhs, lanes,
    points_ref, scale_in, targets_ref, noise_in,
    base_ref, step_ref, along_ref, kept_ref, image_ref,
    raw, scale_ref, noise_ref, zplane, zline, tplane, tline, part, wplane, wline, part2, tiny, tiny2, khi, klo, held,
    load_sem, send_sem, recv_sem,
):
    r, c = lax.axis_index("row"), lax.axis_index("col")
    every = nr * nc

    def turn(position, k, count):
        moved = position + k
        return jnp.where(moved >= count, moved - count, moved)

    rows = [r] + [turn(r, k, nr) for k in range(1, nr)] if every <= 32 else None
    cols = [c] + [turn(c, k, nc) for k in range(1, nc)] if every <= 32 else None

    def at(kr, kc):
        if rows is not None:
            return (rows[kr], cols[kc])
        return (turn(r, kr, nr), turn(c, kc, nc))

    barrier = pltpu.get_barrier_semaphore()
    loop(1, nr, lambda k: pl.semaphore_signal(barrier, inc=1, device_id=at(k, 0), device_id_type=MESH))
    loop(1, nc, lambda k: pl.semaphore_signal(barrier, inc=1, device_id=at(0, k), device_id_type=MESH))
    loads = [
        pltpu.make_async_copy(src, dst, load_sem.at[i])
        for i, (src, dst) in enumerate([
            (points_ref, raw), (scale_in, scale_ref), (targets_ref, tplane.at[0]),
            (targets_ref, tline.at[0]), (noise_in, noise_ref),
        ])
    ]
    for load in loads:
        load.start()
    loads[0].wait()
    loads[1].wait()
    scaled = raw[...] * column(scale_ref, feats, lanes)
    zplane[0] = scaled
    zline[0] = scaled
    for load in loads[2:]:
        load.wait()
    pl.semaphore_wait(barrier, nr + nc - 2)

    class Group:
        count = 0

        def __init__(self, ref, last, peer, src=lambda k: 0):
            self.ref, self.last, self.peer, self.src = ref, last, peer, src
            self.sem = Group.count
            Group.count += 1

        def start(self, low=1, high=None):
            def one(k):
                pltpu.make_async_remote_copy(
                    src_ref=self.ref.at[self.src(k)], dst_ref=self.ref.at[k],
                    send_sem=send_sem.at[self.sem], recv_sem=recv_sem.at[self.sem],
                    device_id=self.peer(k), device_id_type=MESH,
                ).start()

            loop(low, self.last if high is None else high, one)

        def wait(self, sem):
            slots = self.ref.at[pl.ds(1, self.last - 1)]
            pltpu.make_async_copy(slots, slots, sem.at[self.sem]).wait()

        def arrived(self):
            self.wait(recv_sem)

        def sent(self):
            self.wait(send_sem)

    along_col = lambda k: at(0, k)
    along_row = lambda k: at(k, 0)
    back_col = lambda k: at(0, nc - k)
    anywhere = lambda k: at(k // nc, k % nc)
    z_line = Group(zline, nc, along_col)
    z_plane = Group(zplane, nr, along_row)
    t_line = Group(tline, nc, along_col)
    t_plane = Group(tplane, nr, along_row)
    give = Group(part, nc, back_col, lambda k: nc + k)
    w_line = Group(wline, nc, along_col)
    w_plane = Group(wplane, nr, along_row)
    scalars = Group(tiny, every, anywhere)
    give2 = Group(part2, nc, back_col, lambda k: nc + k)
    scalars2 = Group(tiny2, every, anywhere)

    z_line.start()
    z_plane.start()
    t_plane.start()
    t_line.start()

    pair = 2 if nr % 2 == 0 else 1
    steps = nr // pair
    wide = 2 if nc % 2 == 0 else 1
    order = list(range(1, nc)) + [0]
    order = [order[i : i + wide] for i in range(0, nc, wide)]
    few = steps <= FEW

    def cached(make):
        held = {}

        def get(step):
            if not few:
                return make(step)
            if step not in held:
                held[step] = make(step)
            return held[step]

        return get

    def total(body):
        out = jnp.zeros((rhs, wide * lanes), jnp.float32)
        if few:
            for step in range(steps):
                out = body(step, out)
            return out
        return lax.fori_loop(0, steps, body, out)

    def apply(v, high, low):
        both = jnp.dot(v, high, preferred_element_type=jnp.float32)
        return both[:rhs] + both[rhs:] + jnp.dot(v, low, preferred_element_type=jnp.float32)[:rhs]

    def hand_out(columns, partial, ref, group):
        for i, k in enumerate(columns):
            ref[nc + k] = partial[:, i * lanes : (i + 1) * lanes]
            if k:
                group.start(k, k + 1)

    def across(read):
        return lambda step: jnp.concatenate([read(step * pair + k) for k in range(pair)], axis=1)

    z_of = across(lambda k: zplane[k])
    t_of = across(lambda k: tplane[k])
    left = cached(lambda step: factors(z_of(step), True).T.astype(jnp.bfloat16))
    first_v = cached(lambda step: two(t_of(step)))

    z_line.arrived()
    rights = [
        factors(jnp.concatenate([zline[k] for k in columns], axis=1), False).astype(jnp.bfloat16)
        for columns in order
    ]
    z_plane.arrived()

    def low_part(tile):
        return (tile - tile.astype(jnp.bfloat16).astype(jnp.float32)).astype(jnp.bfloat16)

    def make_tile(i, step):
        tile = jnp.exp2(jnp.dot(left(step), rights[i], preferred_element_type=jnp.float32))
        high = tile.astype(jnp.bfloat16)
        khi[i, step] = high
        if few:
            held[i, step] = tile
        else:
            klo[i, step] = low_part(tile)
        return high

    def first(i, step, out, high):
        both = jnp.dot(first_v(step), high, preferred_element_type=jnp.float32)
        return out + both[:rhs] + both[rhs:]

    for i, columns in enumerate(order):
        if few and i == 0:
            for step in range(steps):
                make_tile(i, step)
            t_plane.arrived()
            partial = total(lambda step, out: first(i, step, out, khi[i, step]))
        else:
            if i == 0:
                t_plane.arrived()
            partial = total(lambda step, out: first(i, step, out, make_tile(i, step)))
        hand_out(columns, partial, part, give)
    if few:
        for i in range(len(order)):
            for step in range(steps):
                klo[i, step] = low_part(held[i, step])

    noise = column(noise_ref, rhs, lanes)
    target = tplane[0]
    image = part[nc] + noise * target
    give.arrived()
    for k in range(1, nc):
        image = image + part[k]

    wplane[0] = image
    wline[0] = image
    w_plane.start()
    tiny[0] = lane_sums([target * target, target * image, image * image])
    scalars.start()
    w_line.start()
    w_plane.arrived()
    scalars.arrived()

    sums = to_column(jnp.sum(tiny[...], axis=0))
    tt, tw, ww = sums[:rhs], sums[rhs : 2 * rhs], sums[2 * rhs : 3 * rhs]
    alpha = tt / tw
    beta = alpha * alpha * ww / tt - 1.0

    def direct(t, w):
        return (t - alpha * w) + beta * t

    d_of = across(lambda k: direct(tplane[k], wplane[k]))
    second_v = cached(lambda step: two(d_of(step)))
    residual = target - alpha * image
    direction = direct(target, image)
    curved = noise * direction * direction
    for i, columns in enumerate(order):
        partial = total(lambda step, out: out + apply(second_v(step), khi[i, step], klo[i, step]))
        hand_out(columns, partial, part2, give2)
        if i == 0:
            w_line.arrived()
            t_line.arrived()
        for k in columns:
            curved = curved + direct(tline[k], wline[k]) * part2[nc + k]
    tiny2[0] = lane_sums([curved, residual * residual])
    scalars2.start()
    base_ref[...] = alpha * target
    along_ref[...] = direction
    kept_ref[...] = residual
    image2 = part2[nc] + noise * direction
    give2.arrived()
    for k in range(1, nc):
        image2 = image2 + part2[k]
    image_ref[...] = image2
    scalars2.arrived()
    sums = to_column(jnp.sum(tiny2[...], axis=0))
    alpha2 = sums[rhs : 2 * rhs] / sums[:rhs]
    step_ref[...] = jnp.broadcast_to(alpha2, (rhs, lanes))
    for g in (z_line, z_plane, t_plane, t_line, give, w_line, w_plane, scalars, give2, scalars2):
        g.sent()


def solution(mesh):
    nr, nc = mesh.shape["row"], mesh.shape["col"]

    def on_device(points, inverse_scale, targets, noise_var):
        feats, lanes = points.shape
        rhs = targets.shape[0]
        pair = 2 if nr % 2 == 0 else 1
        wide = 2 if nc % 2 == 0 else 1
        every = nr * nc
        f32 = jnp.float32
        dma = pltpu.SemaphoreType.DMA
        tiles = (nc // wide, nr // pair, pair * lanes, wide * lanes)
        anywhere = pl.BlockSpec(memory_space=pl.ANY)
        base, step, along, kept, image = pl.pallas_call(
            functools.partial(kernel, nr, nc, feats, rhs, lanes),
            out_shape=(pltpu.VMEM((rhs, lanes), f32),) * 5,
            in_specs=[anywhere] * 4,
            out_specs=(pl.BlockSpec(memory_space=pltpu.VMEM),) * 5,
            scratch_shapes=[
                pltpu.VMEM((feats, lanes), f32),
                pltpu.SMEM((feats,), f32),
                pltpu.SMEM((rhs,), f32),
                pltpu.VMEM((nr, feats, lanes), f32),
                pltpu.VMEM((nc, feats, lanes), f32),
                pltpu.VMEM((nr, rhs, lanes), f32),
                pltpu.VMEM((nc, rhs, lanes), f32),
                pltpu.VMEM((2 * nc, rhs, lanes), f32),
                pltpu.VMEM((nr, rhs, lanes), f32),
                pltpu.VMEM((nc, rhs, lanes), f32),
                pltpu.VMEM((2 * nc, rhs, lanes), f32),
                pltpu.VMEM((every, 1, lanes), f32),
                pltpu.VMEM((every, 1, lanes), f32),
                pltpu.VMEM(tiles, jnp.bfloat16),
                pltpu.VMEM(tiles, jnp.bfloat16),
                pltpu.VMEM(tiles if nr // pair <= FEW else (8, 128), f32),
                dma((5,)),
                dma((10,)),
                dma((10,)),
            ],
            compiler_params=pltpu.CompilerParams(
                collective_id=0, has_side_effects=True, vmem_limit_bytes=56 * 1024 * 1024
            ),
        )(points, inverse_scale, targets, noise_var)
        return base + step * along, kept - step * image

    spec = P(None, ("row", "col"))
    return jax.shard_map(
        on_device, mesh=mesh, in_specs=(spec, P(), spec, P()), out_specs=(spec, spec), check_vma=False
    )
```

```python
import functools
import math
import jax
import jax.numpy as jnp
from jax import lax
from jax.experimental import pallas as pl
from jax.experimental.pallas import tpu as pltpu
from jax.sharding import PartitionSpec as P

FEW = 8
MESH = pl.DeviceIdType.MESH
ROOT = math.sqrt(1.0 / math.log(2.0))


def loop(low, high, body):
    if high - low <= 32:
        for k in range(low, high):
            body(k)
    else:

        def step(k, carry):
            body(k)
            return carry

        lax.fori_loop(low, high, step, 0)


def three(x):
    high = x.astype(jnp.bfloat16).astype(jnp.float32)
    rest = x - high
    middle = rest.astype(jnp.bfloat16).astype(jnp.float32)
    return high, middle, rest - middle


def two(x):
    high = x.astype(jnp.bfloat16)
    low = (x - high.astype(jnp.float32)).astype(jnp.bfloat16)
    return jnp.concatenate([high, low], axis=0)


def factors(z, left):
    z = z * ROOT
    half = 0.5 * jnp.sum(z * z, axis=0, keepdims=True)
    h, m, l = three(z)
    a, b, c = three(-half)
    row = lax.broadcasted_iota(jnp.int32, z.shape, 0)
    norms = jnp.where(row == 0, a, jnp.where(row == 1, b, jnp.where(row == 2, c, 0.0)))
    ones = jnp.ones_like(z)
    parts = [h, h, m, h, l, m, norms, ones] if left else [h, m, h, l, h, m, ones, norms]
    return jnp.concatenate(parts, axis=0)


def column(ref, count, lanes):
    row = lax.broadcasted_iota(jnp.int32, (count, lanes), 0)
    out = jnp.zeros((count, lanes), jnp.float32)
    for k in range(count):
        out = jnp.where(row == k, ref[k], out)
    return out


def lane_sums(parts):
    used = sum(p.shape[0] for p in parts)
    parts = parts + [jnp.zeros((128 - used, 128), jnp.float32)]
    return jnp.sum(jnp.concatenate(parts, axis=0).T, axis=0, keepdims=True)


def to_column(row):
    return jnp.broadcast_to(row, (128, 128)).T


def kernel(
    nr, nc, feats, rhs, lanes,
    points_ref, scale_in, targets_ref, noise_in,
    base_ref, step_ref, along_ref, kept_ref, image_ref,
    raw, scale_ref, noise_ref, zplane, zline, tplane, tline, part, wplane, wline, part2, early, tiny, khi, klo, held,
    load_sem, send_sem, recv_sem,
):
    r, c = lax.axis_index("row"), lax.axis_index("col")
    every = nr * nc

    def turn(position, k, count):
        moved = position + k
        return jnp.where(moved >= count, moved - count, moved)

    rows = [r] + [turn(r, k, nr) for k in range(1, nr)] if every <= 32 else None
    cols = [c] + [turn(c, k, nc) for k in range(1, nc)] if every <= 32 else None

    def at(kr, kc):
        if rows is not None:
            return (rows[kr], cols[kc])
        return (turn(r, kr, nr), turn(c, kc, nc))

    barrier = pltpu.get_barrier_semaphore()
    loop(1, nr, lambda k: pl.semaphore_signal(barrier, inc=1, device_id=at(k, 0), device_id_type=MESH))
    loop(1, nc, lambda k: pl.semaphore_signal(barrier, inc=1, device_id=at(0, k), device_id_type=MESH))
    loads = [
        pltpu.make_async_copy(src, dst, load_sem.at[i])
        for i, (src, dst) in enumerate([
            (points_ref, raw), (scale_in, scale_ref), (targets_ref, tplane.at[0]),
            (targets_ref, tline.at[0]), (noise_in, noise_ref),
        ])
    ]
    for load in loads:
        load.start()
    loads[0].wait()
    loads[1].wait()
    scaled = raw[...] * column(scale_ref, feats, lanes)
    zplane[0] = scaled
    zline[0] = scaled
    for load in loads[2:]:
        load.wait()
    pl.semaphore_wait(barrier, nr + nc - 2)

    class Group:
        count = 0

        def __init__(self, ref, last, peer, src=lambda k: 0):
            self.ref, self.last, self.peer, self.src = ref, last, peer, src
            self.sem = Group.count
            Group.count += 1

        def start(self, low=1, high=None):
            def one(k):
                pltpu.make_async_remote_copy(
                    src_ref=self.ref.at[self.src(k)], dst_ref=self.ref.at[k],
                    send_sem=send_sem.at[self.sem], recv_sem=recv_sem.at[self.sem],
                    device_id=self.peer(k), device_id_type=MESH,
                ).start()

            loop(low, self.last if high is None else high, one)

        def wait(self, sem):
            slots = self.ref.at[pl.ds(1, self.last - 1)]
            pltpu.make_async_copy(slots, slots, sem.at[self.sem]).wait()

        def arrived(self):
            self.wait(recv_sem)

        def sent(self):
            self.wait(send_sem)

    along_col = lambda k: at(0, k)
    along_row = lambda k: at(k, 0)
    back_col = lambda k: at(0, nc - k)
    anywhere = lambda k: at(k // nc, k % nc)
    z_line = Group(zline, nc, along_col)
    z_plane = Group(zplane, nr, along_row)
    t_line = Group(tline, nc, along_col)
    t_plane = Group(tplane, nr, along_row)
    give = Group(part, nc, back_col, lambda k: nc + k)
    w_line = Group(wline, nc, along_col)
    w_plane = Group(wplane, nr, along_row)
    scalars = Group(early, nc, along_col)
    give2 = Group(part2, nc, back_col, lambda k: nc + k)
    scalars2 = Group(tiny, every, anywhere)

    z_line.start()
    z_plane.start()
    t_plane.start()
    t_line.start()

    pair = 2 if nr % 2 == 0 else 1
    steps = nr // pair
    wide = 2 if nc % 2 == 0 else 1
    order = list(range(1, nc)) + [0]
    order = [order[i : i + wide] for i in range(0, nc, wide)]
    few = steps <= FEW

    def cached(make):
        held = {}

        def get(step):
            if not few:
                return make(step)
            if step not in held:
                held[step] = make(step)
            return held[step]

        return get

    def total(body):
        out = jnp.zeros((rhs, wide * lanes), jnp.float32)
        if few:
            for step in range(steps):
                out = body(step, out)
            return out
        return lax.fori_loop(0, steps, body, out)

    def apply(v, high, low):
        both = jnp.dot(v, high, preferred_element_type=jnp.float32)
        return both[:rhs] + both[rhs:] + jnp.dot(v, low, preferred_element_type=jnp.float32)[:rhs]

    def hand_out(columns, partial, ref, group):
        for i, k in enumerate(columns):
            ref[nc + k] = partial[:, i * lanes : (i + 1) * lanes]
            if k:
                group.start(k, k + 1)

    def across(read):
        return lambda step: jnp.concatenate([read(step * pair + k) for k in range(pair)], axis=1)

    z_of = across(lambda k: zplane[k])
    t_of = across(lambda k: tplane[k])
    left = cached(lambda step: factors(z_of(step), True).T.astype(jnp.bfloat16))
    first_v = cached(lambda step: two(t_of(step)))

    z_line.arrived()
    rights = [
        factors(jnp.concatenate([zline[k] for k in columns], axis=1), False).astype(jnp.bfloat16)
        for columns in order
    ]
    z_plane.arrived()

    def low_part(tile):
        return (tile - tile.astype(jnp.bfloat16).astype(jnp.float32)).astype(jnp.bfloat16)

    def make_tile(i, step):
        tile = jnp.exp2(jnp.dot(left(step), rights[i], preferred_element_type=jnp.float32))
        high = tile.astype(jnp.bfloat16)
        khi[i, step] = high
        if few:
            held[i, step] = tile
        else:
            klo[i, step] = low_part(tile)
        return high

    def first(i, step, out, high):
        both = jnp.dot(first_v(step), high, preferred_element_type=jnp.float32)
        return out + both[:rhs] + both[rhs:]

    for i, columns in enumerate(order):
        if few and i == 0:
            for step in range(steps):
                make_tile(i, step)
            t_plane.arrived()
            partial = total(lambda step, out: first(i, step, out, khi[i, step]))
        else:
            if i == 0:
                t_plane.arrived()
            partial = total(lambda step, out: first(i, step, out, make_tile(i, step)))
        hand_out(columns, partial, part, give)
    target = tplane[0]
    t_line.arrived()
    along, squared = jnp.zeros((rhs, lanes), jnp.float32), jnp.zeros((rhs, lanes), jnp.float32)
    for k in range(nc):
        along = along + tline[k] * part[nc + k]
        squared = squared + part[nc + k] * part[nc + k]
    early[0] = lane_sums([along, squared, target * target])
    scalars.start()
    if few:
        for i in range(len(order)):
            for step in range(steps):
                klo[i, step] = low_part(held[i, step])

    noise = column(noise_ref, rhs, lanes)
    image = part[nc] + noise * target
    give.arrived()
    for k in range(1, nc):
        image = image + part[k]

    scalars.arrived()
    wplane[0, 0:rhs, :] = image
    wplane[0, rhs : rhs + 8, :] = jnp.broadcast_to(jnp.sum(early[...], axis=0), (8, lanes))
    wline[0] = image
    w_plane.start()
    w_line.start()
    w_plane.arrived()

    row = wplane[0, rhs : rhs + 8, :]
    for k in range(1, nr):
        row = row + wplane[k, rhs : rhs + 8, :]
    sums = to_column(row[0:1])
    tkt, spread, tt = sums[:rhs], sums[rhs : 2 * rhs], sums[2 * rhs : 3 * rhs]
    tw = tkt + noise * tt
    alpha = tt / tw
    guess = alpha * alpha * (nc * spread + 2.0 * noise * tkt + noise * noise * tt) / tt - 1.0

    def direct(t, w):
        return (t - alpha * w) + guess * t

    d_of = across(lambda k: direct(tplane[k], wplane[k, 0:rhs, :]))
    second_v = cached(lambda step: two(d_of(step)))
    residual = target - alpha * image
    direction = direct(target, image)
    curved = noise * direction * direction
    for i, columns in enumerate(order):
        partial = total(lambda step, out: out + apply(second_v(step), khi[i, step], klo[i, step]))
        hand_out(columns, partial, part2, give2)
        if i == 0:
            w_line.arrived()
        for k in columns:
            curved = curved + direct(tline[k], wline[k]) * part2[nc + k]
    tiny[0] = lane_sums([curved, residual * residual, direction * image])
    scalars2.start()
    base_ref[...] = alpha * target
    kept_ref[...] = residual
    image2 = part2[nc] + noise * direction
    give2.arrived()
    for k in range(1, nc):
        image2 = image2 + part2[k]
    scalars2.arrived()
    sums = to_column(jnp.sum(tiny[...], axis=0))
    curvature, norm, mixed = sums[:rhs], sums[rhs : 2 * rhs], sums[2 * rhs : 3 * rhs]
    missed = norm / tt - guess
    step_ref[...] = norm / (curvature + 2.0 * missed * mixed + missed * missed * tw)
    along_ref[...] = direction + missed * target
    image_ref[...] = image2 + missed * image
    for g in (z_line, z_plane, t_plane, t_line, give, w_line, w_plane, scalars, give2, scalars2):
        g.sent()


def solution(mesh):
    nr, nc = mesh.shape["row"], mesh.shape["col"]

    def on_device(points, inverse_scale, targets, noise_var):
        feats, lanes = points.shape
        rhs = targets.shape[0]
        pair = 2 if nr % 2 == 0 else 1
        wide = 2 if nc % 2 == 0 else 1
        every = nr * nc
        f32 = jnp.float32
        dma = pltpu.SemaphoreType.DMA
        tiles = (nc // wide, nr // pair, pair * lanes, wide * lanes)
        anywhere = pl.BlockSpec(memory_space=pl.ANY)
        base, step, along, kept, image = pl.pallas_call(
            functools.partial(kernel, nr, nc, feats, rhs, lanes),
            out_shape=(pltpu.VMEM((rhs, lanes), f32),) * 5,
            in_specs=[anywhere] * 4,
            out_specs=(pl.BlockSpec(memory_space=pltpu.VMEM),) * 5,
            scratch_shapes=[
                pltpu.VMEM((feats, lanes), f32),
                pltpu.SMEM((feats,), f32),
                pltpu.SMEM((rhs,), f32),
                pltpu.VMEM((nr, feats, lanes), f32),
                pltpu.VMEM((nc, feats, lanes), f32),
                pltpu.VMEM((nr, rhs, lanes), f32),
                pltpu.VMEM((nc, rhs, lanes), f32),
                pltpu.VMEM((2 * nc, rhs, lanes), f32),
                pltpu.VMEM((nr, rhs + 8, lanes), f32),
                pltpu.VMEM((nc, rhs, lanes), f32),
                pltpu.VMEM((2 * nc, rhs, lanes), f32),
                pltpu.VMEM((nc, 1, lanes), f32),
                pltpu.VMEM((every, 1, lanes), f32),
                pltpu.VMEM(tiles, jnp.bfloat16),
                pltpu.VMEM(tiles, jnp.bfloat16),
                pltpu.VMEM(tiles if nr // pair <= FEW else (8, 128), f32),
                dma((5,)),
                dma((10,)),
                dma((10,)),
            ],
            compiler_params=pltpu.CompilerParams(
                collective_id=0, has_side_effects=True, vmem_limit_bytes=56 * 1024 * 1024
            ),
        )(points, inverse_scale, targets, noise_var)
        return base + step * along, kept - step * image

    spec = P(None, ("row", "col"))
    return jax.shard_map(
        on_device, mesh=mesh, in_specs=(spec, P(), spec, P()), out_specs=(spec, spec), check_vma=False
    )
```

```python
import functools
import math
import jax
import jax.numpy as jnp
from jax import lax
from jax.experimental import pallas as pl
from jax.experimental.pallas import tpu as pltpu
from jax.sharding import PartitionSpec as P

FEW = 8
MESH = pl.DeviceIdType.MESH
ROOT = math.sqrt(1.0 / math.log(2.0))


def loop(low, high, body):
    if high - low <= 32:
        for k in range(low, high):
            body(k)
    else:

        def step(k, carry):
            body(k)
            return carry

        lax.fori_loop(low, high, step, 0)


def three(x):
    high = x.astype(jnp.bfloat16).astype(jnp.float32)
    rest = x - high
    middle = rest.astype(jnp.bfloat16).astype(jnp.float32)
    return high, middle, rest - middle


def two(x):
    high = x.astype(jnp.bfloat16)
    low = (x - high.astype(jnp.float32)).astype(jnp.bfloat16)
    return jnp.concatenate([high, low], axis=0)


def factors(z, left):
    z = z * ROOT
    half = 0.5 * jnp.sum(z * z, axis=0, keepdims=True)
    h, m, l = three(z)
    a, b, c = three(-half)
    row = lax.broadcasted_iota(jnp.int32, z.shape, 0)
    norms = jnp.where(row == 0, a, jnp.where(row == 1, b, jnp.where(row == 2, c, 0.0)))
    ones = jnp.ones_like(z)
    parts = [h, h, m, h, l, m, norms, ones] if left else [h, m, h, l, h, m, ones, norms]
    return jnp.concatenate(parts, axis=0)


def column(ref, count, lanes):
    row = lax.broadcasted_iota(jnp.int32, (count, lanes), 0)
    out = jnp.zeros((count, lanes), jnp.float32)
    for k in range(count):
        out = jnp.where(row == k, ref[k], out)
    return out


def lane_sums(parts):
    used = sum(p.shape[0] for p in parts)
    parts = parts + [jnp.zeros((128 - used, 128), jnp.float32)]
    return jnp.sum(jnp.concatenate(parts, axis=0).T, axis=0, keepdims=True)


def to_column(row):
    return jnp.broadcast_to(row, (128, 128)).T


def kernel(
    nr, nc, feats, rhs, lanes,
    points_ref, scale_in, targets_ref, noise_in,
    base_ref, step_ref, along_ref, kept_ref, image_ref,
    raw, scale_ref, noise_ref, zplane, zline, tplane, tline, part, wplane, wline, part2, early, tiny, khi, klo, held,
    load_sem, send_sem, recv_sem, line_sem,
):
    r, c = lax.axis_index("row"), lax.axis_index("col")
    every = nr * nc

    def turn(position, k, count):
        moved = position + k
        return jnp.where(moved >= count, moved - count, moved)

    rows = [r] + [turn(r, k, nr) for k in range(1, nr)] if every <= 32 else None
    cols = [c] + [turn(c, k, nc) for k in range(1, nc)] if every <= 32 else None

    def at(kr, kc):
        if rows is not None:
            return (rows[kr], cols[kc])
        return (turn(r, kr, nr), turn(c, kc, nc))

    barrier = pltpu.get_barrier_semaphore()
    loop(1, nr, lambda k: pl.semaphore_signal(barrier, inc=1, device_id=at(k, 0), device_id_type=MESH))
    loop(1, nc, lambda k: pl.semaphore_signal(barrier, inc=1, device_id=at(0, k), device_id_type=MESH))
    loads = [
        pltpu.make_async_copy(src, dst, load_sem.at[i])
        for i, (src, dst) in enumerate([
            (points_ref, raw), (scale_in, scale_ref), (targets_ref, tplane.at[0]),
            (targets_ref, tline.at[0]), (noise_in, noise_ref),
        ])
    ]
    for load in loads:
        load.start()
    loads[0].wait()
    loads[1].wait()
    scaled = raw[...] * column(scale_ref, feats, lanes)
    zplane[0] = scaled
    zline[0] = scaled
    for load in loads[2:]:
        load.wait()
    pl.semaphore_wait(barrier, nr + nc - 2)

    class Group:
        count = 0

        def __init__(self, ref, last, peer, src=lambda k: 0, slot_sems=None):
            self.ref, self.last, self.peer, self.src = ref, last, peer, src
            self.slot_sems = slot_sems
            self.sem = Group.count
            Group.count += 1

        def start(self, low=1, high=None):
            def one(k):
                arrival = recv_sem.at[self.sem] if self.slot_sems is None else self.slot_sems.at[k]
                pltpu.make_async_remote_copy(
                    src_ref=self.ref.at[self.src(k)], dst_ref=self.ref.at[k],
                    send_sem=send_sem.at[self.sem], recv_sem=arrival,
                    device_id=self.peer(k), device_id_type=MESH,
                ).start()

            loop(low, self.last if high is None else high, one)

        def wait(self, sem):
            slots = self.ref.at[pl.ds(1, self.last - 1)]
            pltpu.make_async_copy(slots, slots, sem.at[self.sem]).wait()

        def wait_slot(self, k):
            pltpu.make_async_copy(self.ref.at[k], self.ref.at[k], self.slot_sems.at[k]).wait()

        def arrived(self):
            self.wait(recv_sem)

        def sent(self):
            self.wait(send_sem)

    along_col = lambda k: at(0, k)
    along_row = lambda k: at(k, 0)
    back_col = lambda k: at(0, nc - k)
    anywhere = lambda k: at(k // nc, k % nc)
    z_line = Group(zline, nc, along_col, slot_sems=line_sem)
    z_plane = Group(zplane, nr, along_row)
    t_line = Group(tline, nc, along_col)
    t_plane = Group(tplane, nr, along_row)
    give = Group(part, nc, back_col, lambda k: nc + k)
    w_line = Group(wline, nc, along_col)
    w_plane = Group(wplane, nr, along_row)
    scalars = Group(early, nc, along_col)
    give2 = Group(part2, nc, back_col, lambda k: nc + k)
    scalars2 = Group(tiny, every, anywhere)

    z_line.start()
    z_plane.start()
    t_plane.start()
    t_line.start()

    pair = 2 if nr % 2 == 0 else 1
    steps = nr // pair
    wide = 2 if nc % 2 == 0 else 1
    order = sorted(range(1, nc), key=lambda k: min(k, nc - k)) + [0]
    order = [order[i : i + wide] for i in range(0, nc, wide)]
    few = steps <= FEW

    def cached(make):
        held = {}

        def get(step):
            if not few:
                return make(step)
            if step not in held:
                held[step] = make(step)
            return held[step]

        return get

    def total(body, width):
        out = jnp.zeros((rhs, width * lanes), jnp.float32)
        if few:
            for step in range(steps):
                out = body(step, out)
            return out
        return lax.fori_loop(0, steps, body, out)

    def apply(v, high, low):
        both = jnp.dot(v, high, preferred_element_type=jnp.float32)
        return both[:rhs] + both[rhs:] + jnp.dot(v, low, preferred_element_type=jnp.float32)[:rhs]

    def hand_out(columns, partial, ref, group):
        for i, k in enumerate(columns):
            ref[nc + k] = partial[:, i * lanes : (i + 1) * lanes]
            if k:
                group.start(k, k + 1)

    def across(read):
        return lambda step: jnp.concatenate([read(step * pair + k) for k in range(pair)], axis=1)

    z_of = across(lambda k: zplane[k])
    t_of = across(lambda k: tplane[k])
    left = cached(lambda step: factors(z_of(step), True).T.astype(jnp.bfloat16))
    first_v = cached(lambda step: two(t_of(step)))

    z_plane.arrived()

    def low_part(tile):
        return (tile - tile.astype(jnp.bfloat16).astype(jnp.float32)).astype(jnp.bfloat16)

    def make_tile(k, right, step):
        tile = jnp.exp2(jnp.dot(left(step), right, preferred_element_type=jnp.float32))
        high = tile.astype(jnp.bfloat16)
        khi[k, step] = high
        if few:
            held[k, step] = tile
        else:
            klo[k, step] = low_part(tile)
        return high

    def first(step, out, high):
        both = jnp.dot(first_v(step), high, preferred_element_type=jnp.float32)
        return out + both[:rhs] + both[rhs:]

    for k in range(nc):
        if k:
            z_line.wait_slot(k)
        right = factors(zline[k], False).astype(jnp.bfloat16)
        if few and k == 0:
            for step in range(steps):
                make_tile(k, right, step)
            t_plane.arrived()
            partial = total(lambda step, out: first(step, out, khi[k, step]), 1)
        else:
            if k == 0:
                t_plane.arrived()
            partial = total(lambda step, out: first(step, out, make_tile(k, right, step)), 1)
        hand_out([k], partial, part, give)
    target = tplane[0]
    t_line.arrived()
    along, squared = jnp.zeros((rhs, lanes), jnp.float32), jnp.zeros((rhs, lanes), jnp.float32)
    for k in range(nc):
        along = along + tline[k] * part[nc + k]
        squared = squared + part[nc + k] * part[nc + k]
    early[0] = lane_sums([along, squared, target * target])
    scalars.start()
    if few:
        for k in range(nc):
            for step in range(steps):
                klo[k, step] = low_part(held[k, step])

    noise = column(noise_ref, rhs, lanes)
    image = part[nc] + noise * target
    give.arrived()
    for k in range(1, nc):
        image = image + part[k]

    scalars.arrived()
    wplane[0, 0:rhs, :] = image
    wplane[0, rhs : rhs + 8, :] = jnp.broadcast_to(jnp.sum(early[...], axis=0), (8, lanes))
    wline[0] = image
    w_plane.start()
    w_line.start()
    w_plane.arrived()

    row = wplane[0, rhs : rhs + 8, :]
    for k in range(1, nr):
        row = row + wplane[k, rhs : rhs + 8, :]
    sums = to_column(row[0:1])
    tkt, spread, tt = sums[:rhs], sums[rhs : 2 * rhs], sums[2 * rhs : 3 * rhs]
    tw = tkt + noise * tt
    alpha = tt / tw
    guess = alpha * alpha * (nc * spread + 2.0 * noise * tkt + noise * noise * tt) / tt - 1.0

    def direct(t, w):
        return (t - alpha * w) + guess * t

    d_of = across(lambda k: direct(tplane[k], wplane[k, 0:rhs, :]))
    second_v = cached(lambda step: two(d_of(step)))
    residual = target - alpha * image
    direction = direct(target, image)
    curved = noise * direction * direction
    for i, columns in enumerate(order):
        beside = lambda ref, step: jnp.concatenate([ref[k, step] for k in columns], axis=1)
        partial = total(
            lambda step, out: out + apply(second_v(step), beside(khi, step), beside(klo, step)), len(columns)
        )
        hand_out(columns, partial, part2, give2)
        if i == 0:
            w_line.arrived()
        for k in columns:
            curved = curved + direct(tline[k], wline[k]) * part2[nc + k]
    tiny[0] = lane_sums([curved, residual * residual, direction * image])
    scalars2.start()
    base_ref[...] = alpha * target
    kept_ref[...] = residual
    image2 = part2[nc] + noise * direction
    give2.arrived()
    for k in range(1, nc):
        image2 = image2 + part2[k]
    scalars2.arrived()
    sums = to_column(jnp.sum(tiny[...], axis=0))
    curvature, norm, mixed = sums[:rhs], sums[rhs : 2 * rhs], sums[2 * rhs : 3 * rhs]
    missed = norm / tt - guess
    step_ref[...] = norm / (curvature + 2.0 * missed * mixed + missed * missed * tw)
    along_ref[...] = direction + missed * target
    image_ref[...] = image2 + missed * image
    for g in (z_line, z_plane, t_plane, t_line, give, w_line, w_plane, scalars, give2, scalars2):
        g.sent()


def solution(mesh):
    nr, nc = mesh.shape["row"], mesh.shape["col"]

    def on_device(points, inverse_scale, targets, noise_var):
        feats, lanes = points.shape
        rhs = targets.shape[0]
        pair = 2 if nr % 2 == 0 else 1
        every = nr * nc
        f32 = jnp.float32
        dma = pltpu.SemaphoreType.DMA
        tiles = (nc, nr // pair, pair * lanes, lanes)
        anywhere = pl.BlockSpec(memory_space=pl.ANY)
        base, step, along, kept, image = pl.pallas_call(
            functools.partial(kernel, nr, nc, feats, rhs, lanes),
            out_shape=(pltpu.VMEM((rhs, lanes), f32),) * 5,
            in_specs=[anywhere] * 4,
            out_specs=(pl.BlockSpec(memory_space=pltpu.VMEM),) * 5,
            scratch_shapes=[
                pltpu.VMEM((feats, lanes), f32),
                pltpu.SMEM((feats,), f32),
                pltpu.SMEM((rhs,), f32),
                pltpu.VMEM((nr, feats, lanes), f32),
                pltpu.VMEM((nc, feats, lanes), f32),
                pltpu.VMEM((nr, rhs, lanes), f32),
                pltpu.VMEM((nc, rhs, lanes), f32),
                pltpu.VMEM((2 * nc, rhs, lanes), f32),
                pltpu.VMEM((nr, rhs + 8, lanes), f32),
                pltpu.VMEM((nc, rhs, lanes), f32),
                pltpu.VMEM((2 * nc, rhs, lanes), f32),
                pltpu.VMEM((nc, 1, lanes), f32),
                pltpu.VMEM((every, 1, lanes), f32),
                pltpu.VMEM(tiles, jnp.bfloat16),
                pltpu.VMEM(tiles, jnp.bfloat16),
                pltpu.VMEM(tiles if nr // pair <= FEW else (8, 128), f32),
                dma((5,)),
                dma((10,)),
                dma((10,)),
                dma((nc,)),
            ],
            compiler_params=pltpu.CompilerParams(
                collective_id=0, has_side_effects=True, vmem_limit_bytes=56 * 1024 * 1024
            ),
        )(points, inverse_scale, targets, noise_var)
        return base + step * along, kept - step * image

    spec = P(None, ("row", "col"))
    return jax.shard_map(
        on_device, mesh=mesh, in_specs=(spec, P(), spec, P()), out_specs=(spec, spec), check_vma=False
    )
```

```python
import functools
import math
import jax
import jax.numpy as jnp
from jax import lax
from jax.experimental import pallas as pl
from jax.experimental.pallas import tpu as pltpu
from jax.sharding import PartitionSpec as P

FEW = 8
MESH = pl.DeviceIdType.MESH
ROOT = math.sqrt(1.0 / math.log(2.0))


def loop(low, high, body):
    if high - low <= 32:
        for k in range(low, high):
            body(k)
    else:

        def step(k, carry):
            body(k)
            return carry

        lax.fori_loop(low, high, step, 0)


def three(x):
    high = x.astype(jnp.bfloat16).astype(jnp.float32)
    rest = x - high
    middle = rest.astype(jnp.bfloat16).astype(jnp.float32)
    return high, middle, rest - middle


def two(x):
    high = x.astype(jnp.bfloat16)
    low = (x - high.astype(jnp.float32)).astype(jnp.bfloat16)
    return jnp.concatenate([high, low], axis=0)


def factors(z, left):
    z = z * ROOT
    half = 0.5 * jnp.sum(z * z, axis=0, keepdims=True)
    h, m, l = three(z)
    a, b, c = three(-half)
    row = lax.broadcasted_iota(jnp.int32, z.shape, 0)
    norms = jnp.where(row == 0, a, jnp.where(row == 1, b, jnp.where(row == 2, c, 0.0)))
    ones = jnp.ones_like(z)
    parts = [h, h, m, h, l, m, norms, ones] if left else [h, m, h, l, h, m, ones, norms]
    return jnp.concatenate(parts, axis=0)


def column(ref, count, lanes):
    row = lax.broadcasted_iota(jnp.int32, (count, lanes), 0)
    out = jnp.zeros((count, lanes), jnp.float32)
    for k in range(count):
        out = jnp.where(row == k, ref[k], out)
    return out


def lane_sums(parts):
    used = sum(p.shape[0] for p in parts)
    parts = parts + [jnp.zeros((128 - used, 128), jnp.float32)]
    return jnp.sum(jnp.concatenate(parts, axis=0).T, axis=0, keepdims=True)


def to_column(row):
    return jnp.broadcast_to(row, (128, 128)).T


def kernel(
    nr, nc, feats, rhs, lanes,
    points_ref, scale_in, targets_ref, noise_in,
    base_ref, step_ref, along_ref, kept_ref, image_ref,
    raw, scale_ref, noise_ref, zplane, zline, tplane, tline, part, wplane, wline, part2, early, tiny, khi, klo, held,
    load_sem, send_sem, recv_sem, line_sem,
):
    r, c = lax.axis_index("row"), lax.axis_index("col")
    every = nr * nc

    def turn(position, k, count):
        moved = position + k
        return jnp.where(moved >= count, moved - count, moved)

    rows = [r] + [turn(r, k, nr) for k in range(1, nr)] if every <= 32 else None
    cols = [c] + [turn(c, k, nc) for k in range(1, nc)] if every <= 32 else None

    def at(kr, kc):
        if rows is not None:
            return (rows[kr], cols[kc])
        return (turn(r, kr, nr), turn(c, kc, nc))

    barrier = pltpu.get_barrier_semaphore()
    loop(1, nr, lambda k: pl.semaphore_signal(barrier, inc=1, device_id=at(k, 0), device_id_type=MESH))
    loop(1, nc, lambda k: pl.semaphore_signal(barrier, inc=1, device_id=at(0, k), device_id_type=MESH))
    loads = [
        pltpu.make_async_copy(src, dst, load_sem.at[i])
        for i, (src, dst) in enumerate([
            (points_ref, raw), (scale_in, scale_ref), (targets_ref, tplane.at[0]),
            (targets_ref, tline.at[0]), (noise_in, noise_ref),
        ])
    ]
    for load in loads:
        load.start()
    loads[0].wait()
    loads[1].wait()
    scaled = raw[...] * column(scale_ref, feats, lanes)
    zplane[0] = scaled
    zline[0] = scaled
    for load in loads[2:]:
        load.wait()
    pl.semaphore_wait(barrier, nr + nc - 2)

    class Group:
        count = 0

        def __init__(self, ref, last, peer, src=lambda k: 0, slot_sems=None):
            self.ref, self.last, self.peer, self.src = ref, last, peer, src
            self.slot_sems = slot_sems
            self.sem = Group.count
            Group.count += 1

        def start(self, low=1, high=None):
            def one(k):
                arrival = recv_sem.at[self.sem] if self.slot_sems is None else self.slot_sems.at[k]
                pltpu.make_async_remote_copy(
                    src_ref=self.ref.at[self.src(k)], dst_ref=self.ref.at[k],
                    send_sem=send_sem.at[self.sem], recv_sem=arrival,
                    device_id=self.peer(k), device_id_type=MESH,
                ).start()

            loop(low, self.last if high is None else high, one)

        def wait(self, sem):
            slots = self.ref.at[pl.ds(1, self.last - 1)]
            pltpu.make_async_copy(slots, slots, sem.at[self.sem]).wait()

        def wait_slot(self, k):
            pltpu.make_async_copy(self.ref.at[k], self.ref.at[k], self.slot_sems.at[k]).wait()

        def arrived(self):
            self.wait(recv_sem)

        def sent(self):
            self.wait(send_sem)

    def across_col(k):
        other, bit = c, 1
        while bit < nc:
            if k & bit:
                other = other + bit * (1 - 2 * lax.rem(lax.div(c, bit), 2))
            bit *= 2
        return (r, other)

    paired = nc & (nc - 1) == 0
    along_col = across_col if paired else lambda k: at(0, k)
    along_row = lambda k: at(k, 0)
    back_col = across_col if paired else lambda k: at(0, nc - k)
    anywhere = lambda k: at(k // nc, k % nc)
    z_line = Group(zline, nc, along_col, slot_sems=line_sem)
    z_plane = Group(zplane, nr, along_row)
    t_line = Group(tline, nc, along_col)
    t_plane = Group(tplane, nr, along_row)
    give = Group(part, nc, back_col, lambda k: nc + k)
    w_line = Group(wline, nc, along_col)
    w_plane = Group(wplane, nr, along_row)
    scalars = Group(early, every, anywhere)
    give2 = Group(part2, nc, back_col, lambda k: nc + k)
    scalars2 = Group(tiny, every, anywhere)

    z_line.start()
    z_plane.start()
    t_plane.start()
    t_line.start()

    pair = 2 if nr % 2 == 0 else 1
    steps = nr // pair
    wide = 2 if nc % 2 == 0 else 1
    order = [list(range(i, i + wide)) for i in range(0, nc, wide)]
    few = steps <= FEW

    def cached(make):
        held = {}

        def get(step):
            if not few:
                return make(step)
            if step not in held:
                held[step] = make(step)
            return held[step]

        return get

    def total(body):
        out = jnp.zeros((rhs, wide * lanes), jnp.float32)
        if few:
            for step in range(steps):
                out = body(step, out)
            return out
        return lax.fori_loop(0, steps, body, out)

    def apply(v, high, low):
        both = jnp.dot(v, high, preferred_element_type=jnp.float32)
        return both[:rhs] + both[rhs:] + jnp.dot(v, low, preferred_element_type=jnp.float32)[:rhs]

    def hand_out(columns, partial, ref, group):
        for i, k in enumerate(columns):
            ref[nc + k] = partial[:, i * lanes : (i + 1) * lanes]
            if k:
                group.start(k, k + 1)

    def across(read):
        return lambda step: jnp.concatenate([read(step * pair + k) for k in range(pair)], axis=1)

    z_of = across(lambda k: zplane[k])
    t_of = across(lambda k: tplane[k])
    left = cached(lambda step: factors(z_of(step), True).T.astype(jnp.bfloat16))
    first_v = cached(lambda step: two(t_of(step)))

    z_plane.arrived()

    def low_part(tile):
        return (tile - tile.astype(jnp.bfloat16).astype(jnp.float32)).astype(jnp.bfloat16)

    def make_tile(i, right, step):
        tile = jnp.exp2(jnp.dot(left(step), right, preferred_element_type=jnp.float32))
        high = tile.astype(jnp.bfloat16)
        khi[i, step] = high
        if few:
            held[i, step] = tile
        else:
            klo[i, step] = low_part(tile)
        return high

    def first(i, step, out, high):
        both = jnp.dot(first_v(step), high, preferred_element_type=jnp.float32)
        return out + both[:rhs] + both[rhs:]

    for i, columns in enumerate(order):
        for k in columns:
            if k:
                z_line.wait_slot(k)
        right = factors(jnp.concatenate([zline[k] for k in columns], axis=1), False).astype(jnp.bfloat16)
        if few and i == 0:
            for step in range(steps):
                make_tile(i, right, step)
            t_plane.arrived()
            partial = total(lambda step, out: first(i, step, out, khi[i, step]))
        else:
            if i == 0:
                t_plane.arrived()
            partial = total(lambda step, out: first(i, step, out, make_tile(i, right, step)))
        hand_out(columns, partial, part, give)
    target = tplane[0]
    t_line.arrived()
    along, squared = jnp.zeros((rhs, lanes), jnp.float32), jnp.zeros((rhs, lanes), jnp.float32)
    for k in range(nc):
        along = along + tline[k] * part[nc + k]
        squared = squared + part[nc + k] * part[nc + k]
    early[0] = lane_sums([along, squared, target * target])
    scalars.start()
    if few:
        for i in range(len(order)):
            for step in range(steps):
                klo[i, step] = low_part(held[i, step])

    noise = column(noise_ref, rhs, lanes)
    image = part[nc] + noise * target
    give.arrived()
    for k in range(1, nc):
        image = image + part[k]

    wplane[0] = image
    wline[0] = image
    w_plane.start()
    w_line.start()
    scalars.arrived()
    sums = to_column(jnp.sum(early[...], axis=0))
    tkt, spread, tt = sums[:rhs], sums[rhs : 2 * rhs], sums[2 * rhs : 3 * rhs]
    tw = tkt + noise * tt
    alpha = tt / tw
    guess = alpha * alpha * (nc * spread + 2.0 * noise * tkt + noise * noise * tt) / tt - 1.0

    w_plane.arrived()

    def direct(t, w):
        return (t - alpha * w) + guess * t

    d_of = across(lambda k: direct(tplane[k], wplane[k]))
    second_v = cached(lambda step: two(d_of(step)))
    residual = target - alpha * image
    direction = direct(target, image)
    curved = noise * direction * direction
    for i, columns in reversed(list(enumerate(order))):
        partial = total(lambda step, out: out + apply(second_v(step), khi[i, step], klo[i, step]))
        hand_out(columns, partial, part2, give2)
        if i == len(order) - 1:
            w_line.arrived()
        for k in columns:
            curved = curved + direct(tline[k], wline[k]) * part2[nc + k]
    tiny[0] = lane_sums([curved, residual * residual, direction * image])
    scalars2.start()
    base_ref[...] = alpha * target
    kept_ref[...] = residual
    image2 = part2[nc] + noise * direction
    give2.arrived()
    for k in range(1, nc):
        image2 = image2 + part2[k]
    scalars2.arrived()
    sums = to_column(jnp.sum(tiny[...], axis=0))
    curvature, norm, mixed = sums[:rhs], sums[rhs : 2 * rhs], sums[2 * rhs : 3 * rhs]
    missed = norm / tt - guess
    step_ref[...] = norm / (curvature + 2.0 * missed * mixed + missed * missed * tw)
    along_ref[...] = direction + missed * target
    image_ref[...] = image2 + missed * image
    for g in (z_line, z_plane, t_plane, t_line, give, w_line, w_plane, scalars, give2, scalars2):
        g.sent()


def solution(mesh):
    nr, nc = mesh.shape["row"], mesh.shape["col"]

    def on_device(points, inverse_scale, targets, noise_var):
        feats, lanes = points.shape
        rhs = targets.shape[0]
        pair = 2 if nr % 2 == 0 else 1
        wide = 2 if nc % 2 == 0 else 1
        every = nr * nc
        f32 = jnp.float32
        dma = pltpu.SemaphoreType.DMA
        tiles = (nc // wide, nr // pair, pair * lanes, wide * lanes)
        anywhere = pl.BlockSpec(memory_space=pl.ANY)
        base, step, along, kept, image = pl.pallas_call(
            functools.partial(kernel, nr, nc, feats, rhs, lanes),
            out_shape=(pltpu.VMEM((rhs, lanes), f32),) * 5,
            in_specs=[anywhere] * 4,
            out_specs=(pl.BlockSpec(memory_space=pltpu.VMEM),) * 5,
            scratch_shapes=[
                pltpu.VMEM((feats, lanes), f32),
                pltpu.SMEM((feats,), f32),
                pltpu.SMEM((rhs,), f32),
                pltpu.VMEM((nr, feats, lanes), f32),
                pltpu.VMEM((nc, feats, lanes), f32),
                pltpu.VMEM((nr, rhs, lanes), f32),
                pltpu.VMEM((nc, rhs, lanes), f32),
                pltpu.VMEM((2 * nc, rhs, lanes), f32),
                pltpu.VMEM((nr, rhs, lanes), f32),
                pltpu.VMEM((nc, rhs, lanes), f32),
                pltpu.VMEM((2 * nc, rhs, lanes), f32),
                pltpu.VMEM((every, 1, lanes), f32),
                pltpu.VMEM((every, 1, lanes), f32),
                pltpu.VMEM(tiles, jnp.bfloat16),
                pltpu.VMEM(tiles, jnp.bfloat16),
                pltpu.VMEM(tiles if nr // pair <= FEW else (8, 128), f32),
                dma((5,)),
                dma((10,)),
                dma((10,)),
                dma((nc,)),
            ],
            compiler_params=pltpu.CompilerParams(
                collective_id=0, has_side_effects=True, vmem_limit_bytes=56 * 1024 * 1024
            ),
        )(points, inverse_scale, targets, noise_var)
        return base + step * along, kept - step * image

    spec = P(None, ("row", "col"))
    return jax.shard_map(
        on_device, mesh=mesh, in_specs=(spec, P(), spec, P()), out_specs=(spec, spec), check_vma=False
    )
```

```python
import functools
import math
import jax
import jax.numpy as jnp
from jax import lax
from jax.experimental import pallas as pl
from jax.experimental.pallas import tpu as pltpu
from jax.sharding import PartitionSpec as P

FEW = 8
MESH = pl.DeviceIdType.MESH
ROOT = math.sqrt(1.0 / math.log(2.0))


def loop(low, high, body, key=None):
    if high - low <= 32:
        for k in sorted(range(low, high), key=key or (lambda k: -k)):
            body(k)
    else:

        def step(k, carry):
            body(k)
            return carry

        lax.fori_loop(low, high, step, 0)


def three(x):
    high = x.astype(jnp.bfloat16).astype(jnp.float32)
    rest = x - high
    middle = rest.astype(jnp.bfloat16).astype(jnp.float32)
    return high, middle, rest - middle


def two(x):
    high = x.astype(jnp.bfloat16)
    low = (x - high.astype(jnp.float32)).astype(jnp.bfloat16)
    return jnp.concatenate([high, low], axis=0)


def factors(z, left):
    z = z * ROOT
    half = 0.5 * jnp.sum(z * z, axis=0, keepdims=True)
    h, m, l = three(z)
    a, b, c = three(-half)
    row = lax.broadcasted_iota(jnp.int32, z.shape, 0)
    norms = jnp.where(row == 0, a, jnp.where(row == 1, b, jnp.where(row == 2, c, 0.0)))
    ones = jnp.ones_like(z)
    parts = [h, h, m, h, l, m, norms, ones] if left else [h, m, h, l, h, m, ones, norms]
    return jnp.concatenate(parts, axis=0)


def column(ref, count, lanes):
    row = lax.broadcasted_iota(jnp.int32, (count, lanes), 0)
    out = jnp.zeros((count, lanes), jnp.float32)
    for k in range(count):
        out = jnp.where(row == k, ref[k], out)
    return out


def lane_sums(parts):
    used = sum(p.shape[0] for p in parts)
    parts = parts + [jnp.zeros((128 - used, 128), jnp.float32)]
    return jnp.sum(jnp.concatenate(parts, axis=0).T, axis=0, keepdims=True)


def to_column(row):
    return jnp.broadcast_to(row, (128, 128)).T


def kernel(
    nr, nc, feats, rhs, lanes,
    points_ref, scale_in, targets_ref, noise_in,
    base_ref, step_ref, along_ref, kept_ref, image_ref,
    raw, scale_ref, noise_ref, zplane, zline, tplane, tline, part, wplane, wline, part2, early, tiny, khi, klo, held,
    load_sem, send_sem, recv_sem, line_sem,
):
    r, c = lax.axis_index("row"), lax.axis_index("col")
    every = nr * nc

    def partner(position, k, count):
        if isinstance(k, int) and count & (count - 1) == 0:
            other, bit = position, 1
            while bit < count:
                if k & bit:
                    other = other + bit * (1 - 2 * lax.rem(lax.div(position, bit), 2))
                bit *= 2
            return other
        moved = position + k
        return jnp.where(moved >= count, moved - count, moved)

    rows = [partner(r, k, nr) for k in range(nr)] if every <= 32 else None
    cols = [partner(c, k, nc) for k in range(nc)] if every <= 32 else None

    def at(kr, kc):
        if rows is not None:
            return (rows[kr], cols[kc])
        return (partner(r, kr, nr), partner(c, kc, nc))

    def distance(k):
        kr, kc = k // nc, k % nc
        return kc + bin(kr // 2).count("1") + 0.5 * (kr % 2)

    barrier = pltpu.get_barrier_semaphore()
    loop(1, nc, lambda k: pl.semaphore_signal(barrier, inc=1, device_id=at(0, k), device_id_type=MESH))
    loop(1, nr, lambda k: pl.semaphore_signal(barrier, inc=1, device_id=at(k, 0), device_id_type=MESH))
    loads = [
        pltpu.make_async_copy(src, dst, load_sem.at[i])
        for i, (src, dst) in enumerate([
            (points_ref, raw), (scale_in, scale_ref), (targets_ref, tplane.at[0]),
            (targets_ref, tline.at[0]), (noise_in, noise_ref),
        ])
    ]
    for load in loads:
        load.start()
    loads[0].wait()
    loads[1].wait()
    scaled = raw[...] * column(scale_ref, feats, lanes)
    zplane[0] = scaled
    zline[0] = scaled
    for load in loads[2:]:
        load.wait()
    pl.semaphore_wait(barrier, nr + nc - 2)

    class Group:
        count = 0

        def __init__(self, ref, last, peer, src=lambda k: 0, slot_sems=None, key=None):
            self.ref, self.last, self.peer, self.src = ref, last, peer, src
            self.slot_sems, self.key = slot_sems, key
            self.sem = Group.count
            Group.count += 1

        def start(self, low=1, high=None):
            def one(k):
                arrival = recv_sem.at[self.sem] if self.slot_sems is None else self.slot_sems.at[k]
                pltpu.make_async_remote_copy(
                    src_ref=self.ref.at[self.src(k)], dst_ref=self.ref.at[k],
                    send_sem=send_sem.at[self.sem], recv_sem=arrival,
                    device_id=self.peer(k), device_id_type=MESH,
                ).start()

            loop(low, self.last if high is None else high, one, self.key)

        def wait(self, sem):
            slots = self.ref.at[pl.ds(1, self.last - 1)]
            pltpu.make_async_copy(slots, slots, sem.at[self.sem]).wait()

        def wait_slot(self, k):
            pltpu.make_async_copy(self.ref.at[k], self.ref.at[k], self.slot_sems.at[k]).wait()

        def arrived(self):
            self.wait(recv_sem)

        def sent(self):
            self.wait(send_sem)

    along_col = lambda k: at(0, k)
    along_row = lambda k: at(k, 0)
    back_col = lambda k: at(0, k if nc & (nc - 1) == 0 else nc - k)
    anywhere = lambda k: at(k // nc, k % nc)
    z_line = Group(zline, nc, along_col, slot_sems=line_sem)
    z_plane = Group(zplane, nr, along_row)
    t_line = Group(tline, nc, along_col)
    t_plane = Group(tplane, nr, along_row)
    give = Group(part, nc, back_col, lambda k: nc + k)
    w_line = Group(wline, nc, along_col)
    w_plane = Group(wplane, nr, along_row)
    scalars = Group(early, every, anywhere, key=lambda k: -distance(k))
    give2 = Group(part2, nc, back_col, lambda k: nc + k)
    scalars2 = Group(tiny, every, anywhere, key=lambda k: -distance(k))

    z_line.start()
    z_plane.start()
    t_plane.start()
    t_line.start()

    pair = 2 if nr % 2 == 0 else 1
    steps = nr // pair
    wide = 2 if nc % 2 == 0 else 1
    order = [list(range(i, i + wide)) for i in range(0, nc, wide)]
    few = steps <= FEW

    def cached(make):
        held = {}

        def get(step):
            if not few:
                return make(step)
            if step not in held:
                held[step] = make(step)
            return held[step]

        return get

    def total(body):
        out = jnp.zeros((rhs, wide * lanes), jnp.float32)
        if few:
            for step in range(steps):
                out = body(step, out)
            return out
        return lax.fori_loop(0, steps, body, out)

    def apply(v, high, low):
        both = jnp.dot(v, high, preferred_element_type=jnp.float32)
        return both[:rhs] + both[rhs:] + jnp.dot(v, low, preferred_element_type=jnp.float32)[:rhs]

    def hand_out(columns, partial, ref, group):
        for i, k in enumerate(columns):
            ref[nc + k] = partial[:, i * lanes : (i + 1) * lanes]
            if k:
                group.start(k, k + 1)

    def across(read):
        return lambda step: jnp.concatenate([read(step * pair + k) for k in range(pair)], axis=1)

    z_of = across(lambda k: zplane[k])
    t_of = across(lambda k: tplane[k])
    left = cached(lambda step: factors(z_of(step), True).T.astype(jnp.bfloat16))
    first_v = cached(lambda step: two(t_of(step)))

    z_plane.arrived()

    def low_part(tile):
        return (tile - tile.astype(jnp.bfloat16).astype(jnp.float32)).astype(jnp.bfloat16)

    def make_tile(i, right, step):
        tile = jnp.exp2(jnp.dot(left(step), right, preferred_element_type=jnp.float32))
        high = tile.astype(jnp.bfloat16)
        khi[i, step] = high
        if few:
            held[i, step] = tile
        else:
            klo[i, step] = low_part(tile)
        return high

    def first(i, step, out, high):
        both = jnp.dot(first_v(step), high, preferred_element_type=jnp.float32)
        return out + both[:rhs] + both[rhs:]

    for i, columns in enumerate(order):
        for k in columns:
            if k:
                z_line.wait_slot(k)
        right = factors(jnp.concatenate([zline[k] for k in columns], axis=1), False).astype(jnp.bfloat16)
        if few and i == 0:
            for step in range(steps):
                make_tile(i, right, step)
            t_plane.arrived()
            partial = total(lambda step, out: first(i, step, out, khi[i, step]))
        else:
            if i == 0:
                t_plane.arrived()
            partial = total(lambda step, out: first(i, step, out, make_tile(i, right, step)))
        hand_out(columns, partial, part, give)
    target = tplane[0]
    t_line.arrived()
    along, squared = jnp.zeros((rhs, lanes), jnp.float32), jnp.zeros((rhs, lanes), jnp.float32)
    for k in range(nc):
        along = along + tline[k] * part[nc + k]
        squared = squared + part[nc + k] * part[nc + k]
    early[0] = lane_sums([along, squared, target * target])
    scalars.start()
    if few:
        for i in range(len(order)):
            for step in range(steps):
                klo[i, step] = low_part(held[i, step])

    noise = column(noise_ref, rhs, lanes)
    image = part[nc] + noise * target
    give.arrived()
    for k in range(1, nc):
        image = image + part[k]

    wplane[0] = image
    wline[0] = image
    w_plane.start()
    w_line.start()
    scalars.arrived()
    sums = to_column(jnp.sum(early[...], axis=0))
    tkt, spread, tt = sums[:rhs], sums[rhs : 2 * rhs], sums[2 * rhs : 3 * rhs]
    tw = tkt + noise * tt
    alpha = tt / tw
    guess = alpha * alpha * (nc * spread + 2.0 * noise * tkt + noise * noise * tt) / tt - 1.0

    w_plane.arrived()

    def direct(t, w):
        return (t - alpha * w) + guess * t

    d_of = across(lambda k: direct(tplane[k], wplane[k]))
    second_v = cached(lambda step: two(d_of(step)))
    residual = target - alpha * image
    direction = direct(target, image)
    curved = noise * direction * direction
    for i, columns in reversed(list(enumerate(order))):
        partial = total(lambda step, out: out + apply(second_v(step), khi[i, step], klo[i, step]))
        hand_out(columns, partial, part2, give2)
        if i == len(order) - 1:
            w_line.arrived()
        for k in columns:
            curved = curved + direct(tline[k], wline[k]) * part2[nc + k]
    tiny[0] = lane_sums([curved, residual * residual, direction * image])
    scalars2.start()
    base_ref[...] = alpha * target
    kept_ref[...] = residual
    image2 = part2[nc] + noise * direction
    give2.arrived()
    for k in range(1, nc):
        image2 = image2 + part2[k]
    scalars2.arrived()
    sums = to_column(jnp.sum(tiny[...], axis=0))
    curvature, norm, mixed = sums[:rhs], sums[rhs : 2 * rhs], sums[2 * rhs : 3 * rhs]
    missed = norm / tt - guess
    step_ref[...] = norm / (curvature + 2.0 * missed * mixed + missed * missed * tw)
    along_ref[...] = direction + missed * target
    image_ref[...] = image2 + missed * image
    for g in (z_line, z_plane, t_plane, t_line, give, w_line, w_plane, scalars, give2, scalars2):
        g.sent()


def solution(mesh):
    nr, nc = mesh.shape["row"], mesh.shape["col"]

    def on_device(points, inverse_scale, targets, noise_var):
        feats, lanes = points.shape
        rhs = targets.shape[0]
        pair = 2 if nr % 2 == 0 else 1
        wide = 2 if nc % 2 == 0 else 1
        every = nr * nc
        f32 = jnp.float32
        dma = pltpu.SemaphoreType.DMA
        tiles = (nc // wide, nr // pair, pair * lanes, wide * lanes)
        anywhere = pl.BlockSpec(memory_space=pl.ANY)
        base, step, along, kept, image = pl.pallas_call(
            functools.partial(kernel, nr, nc, feats, rhs, lanes),
            out_shape=(pltpu.VMEM((rhs, lanes), f32),) * 5,
            in_specs=[anywhere] * 4,
            out_specs=(pl.BlockSpec(memory_space=pltpu.VMEM),) * 5,
            scratch_shapes=[
                pltpu.VMEM((feats, lanes), f32),
                pltpu.SMEM((feats,), f32),
                pltpu.SMEM((rhs,), f32),
                pltpu.VMEM((nr, feats, lanes), f32),
                pltpu.VMEM((nc, feats, lanes), f32),
                pltpu.VMEM((nr, rhs, lanes), f32),
                pltpu.VMEM((nc, rhs, lanes), f32),
                pltpu.VMEM((2 * nc, rhs, lanes), f32),
                pltpu.VMEM((nr, rhs, lanes), f32),
                pltpu.VMEM((nc, rhs, lanes), f32),
                pltpu.VMEM((2 * nc, rhs, lanes), f32),
                pltpu.VMEM((every, 1, lanes), f32),
                pltpu.VMEM((every, 1, lanes), f32),
                pltpu.VMEM(tiles, jnp.bfloat16),
                pltpu.VMEM(tiles, jnp.bfloat16),
                pltpu.VMEM(tiles if nr // pair <= FEW else (8, 128), f32),
                dma((5,)),
                dma((10,)),
                dma((10,)),
                dma((nc,)),
            ],
            compiler_params=pltpu.CompilerParams(
                collective_id=0, has_side_effects=True, vmem_limit_bytes=56 * 1024 * 1024
            ),
        )(points, inverse_scale, targets, noise_var)
        return base + step * along, kept - step * image

    spec = P(None, ("row", "col"))
    return jax.shard_map(
        on_device, mesh=mesh, in_specs=(spec, P(), spec, P()), out_specs=(spec, spec), check_vma=False
    )
```

```python
import functools
import math
import jax
import jax.numpy as jnp
from jax import lax
from jax.experimental import pallas as pl
from jax.experimental.pallas import tpu as pltpu
from jax.sharding import PartitionSpec as P

FEW = 8
MESH = pl.DeviceIdType.MESH
ROOT = math.sqrt(1.0 / math.log(2.0))


def loop(low, high, body, key=None):
    if high - low <= 32:
        for k in sorted(range(low, high), key=key or (lambda k: -k)):
            body(k)
    else:

        def step(k, carry):
            body(k)
            return carry

        lax.fori_loop(low, high, step, 0)


def three(x):
    high = x.astype(jnp.bfloat16).astype(jnp.float32)
    rest = x - high
    middle = rest.astype(jnp.bfloat16).astype(jnp.float32)
    return high, middle, rest - middle


def two(x):
    high = x.astype(jnp.bfloat16)
    low = (x - high.astype(jnp.float32)).astype(jnp.bfloat16)
    return jnp.concatenate([high, low], axis=0)


def factors(z, left):
    z = z * ROOT
    half = 0.5 * jnp.sum(z * z, axis=0, keepdims=True)
    h, m, l = three(z)
    a, b, c = three(-half)
    row = lax.broadcasted_iota(jnp.int32, z.shape, 0)
    norms = jnp.where(row == 0, a, jnp.where(row == 1, b, jnp.where(row == 2, c, 0.0)))
    ones = jnp.ones_like(z)
    parts = [h, h, m, h, l, m, norms, ones] if left else [h, m, h, l, h, m, ones, norms]
    return jnp.concatenate(parts, axis=0)


def column(ref, count, lanes):
    row = lax.broadcasted_iota(jnp.int32, (count, lanes), 0)
    out = jnp.zeros((count, lanes), jnp.float32)
    for k in range(count):
        out = jnp.where(row == k, ref[k], out)
    return out


def lane_sums(parts):
    used = sum(p.shape[0] for p in parts)
    parts = parts + [jnp.zeros((128 - used, 128), jnp.float32)]
    return jnp.sum(jnp.concatenate(parts, axis=0).T, axis=0, keepdims=True)


def to_column(row):
    return jnp.broadcast_to(row, (128, 128)).T


def kernel(
    nr, nc, feats, rhs, lanes,
    points_ref, scale_in, targets_ref, noise_in,
    base_ref, step_ref, along_ref, kept_ref, image_ref,
    raw, scale_ref, noise_ref, zplane, tplane, line, part, wplane, wline, part2, early, tiny, khi, klo, held,
    load_sem, send_sem, recv_sem, line_sem, line_send,
):
    r, c = lax.axis_index("row"), lax.axis_index("col")
    every = nr * nc

    def partner(position, k, count):
        if isinstance(k, int) and count & (count - 1) == 0:
            other, bit = position, 1
            while bit < count:
                if k & bit:
                    other = other + bit * (1 - 2 * lax.rem(lax.div(position, bit), 2))
                bit *= 2
            return other
        moved = position + k
        return jnp.where(moved >= count, moved - count, moved)

    rows = [partner(r, k, nr) for k in range(nr)] if every <= 32 else None
    cols = [partner(c, k, nc) for k in range(nc)] if every <= 32 else None

    def at(kr, kc):
        if rows is not None:
            return (rows[kr], cols[kc])
        return (partner(r, kr, nr), partner(c, kc, nc))

    def distance(k):
        kr, kc = k // nc, k % nc
        return kc + bin(kr // 2).count("1") + 0.5 * (kr % 2)

    barrier = pltpu.get_barrier_semaphore()
    top = nc - 1

    def enter(col):
        pl.semaphore_signal(barrier, inc=1, device_id=(r, col), device_id_type=MESH)

    pl.when(c > 0)(lambda: enter(c - 1))
    for d in range(top, 0, -1):
        pl.when(c + d < nc)(lambda d=d: enter(c + d))
    loop(1, nr, lambda k: pl.semaphore_signal(barrier, inc=1, device_id=at(k, 0), device_id_type=MESH))
    loads = [
        pltpu.make_async_copy(src, dst, load_sem.at[i])
        for i, (src, dst) in enumerate([
            (points_ref, raw), (scale_in, scale_ref), (targets_ref, tplane.at[0]),
            (targets_ref, line.at[c, pl.ds(feats, rhs)]), (noise_in, noise_ref),
        ])
    ]
    for load in loads:
        load.start()
    loads[0].wait()
    loads[1].wait()
    scaled = raw[...] * column(scale_ref, feats, lanes)
    zplane[0] = scaled
    line[c, 0:feats, :] = scaled
    for load in loads[2:]:
        load.wait()
    pl.semaphore_wait(barrier, nr - 1 + c + jnp.where(c < top, 1, 0))

    class Group:
        count = 0

        def __init__(self, ref, last, peer, src=lambda k: 0, slot_sems=None, key=None):
            self.ref, self.last, self.peer, self.src = ref, last, peer, src
            self.slot_sems, self.key = slot_sems, key
            self.sem = Group.count
            Group.count += 1

        def start(self, low=1, high=None):
            def one(k):
                arrival = recv_sem.at[self.sem] if self.slot_sems is None else self.slot_sems.at[k]
                pltpu.make_async_remote_copy(
                    src_ref=self.ref.at[self.src(k)], dst_ref=self.ref.at[k],
                    send_sem=send_sem.at[self.sem], recv_sem=arrival,
                    device_id=self.peer(k), device_id_type=MESH,
                ).start()

            loop(low, self.last if high is None else high, one, self.key)

        def wait(self, sem):
            slots = self.ref.at[pl.ds(1, self.last - 1)]
            pltpu.make_async_copy(slots, slots, sem.at[self.sem]).wait()

        def wait_slot(self, k):
            pltpu.make_async_copy(self.ref.at[k], self.ref.at[k], self.slot_sems.at[k]).wait()

        def arrived(self):
            self.wait(recv_sem)

        def sent(self):
            self.wait(send_sem)

    along_col = lambda k: at(0, k)
    along_row = lambda k: at(k, 0)
    back_col = lambda k: at(0, k if nc & (nc - 1) == 0 else nc - k)
    anywhere = lambda k: at(k // nc, k % nc)
    z_plane = Group(zplane, nr, along_row)
    t_plane = Group(tplane, nr, along_row)
    give = Group(part, nc, along_col, lambda k: nc + k)
    w_line = Group(wline, nc, back_col)
    w_plane = Group(wplane, nr, along_row)
    scalars = Group(early, every, anywhere, key=lambda k: -distance(k))
    give2 = Group(part2, nc, along_col, lambda k: nc + k)
    scalars2 = Group(tiny, every, anywhere, key=lambda k: -distance(k))

    def hop(source, col, slot):
        return pltpu.make_async_remote_copy(
            src_ref=line.at[source], dst_ref=line.at[source], send_sem=line_send.at[slot],
            recv_sem=line_sem.at[source], device_id=(r, col), device_id_type=MESH,
        )

    def landed(source):
        pltpu.make_async_copy(line.at[source], line.at[source], line_sem.at[source]).wait()

    def pass_on(d):
        landed(c - d)
        hop(c - d, c + 1, d).start()

    pl.when(c < top)(lambda: hop(c, c + 1, 0).start())
    for d in range(top, 0, -1):
        pl.when(c >= d)(lambda d=d: hop(c, c - d, nc + d).start())
    z_plane.start()
    t_plane.start()
    for d in range(1, nc):
        pl.when((c >= d) & (c < top))(lambda d=d: pass_on(d))

    def col_of(k):
        return at(0, k)[1]

    pair = 2 if nr % 2 == 0 else 1
    steps = nr // pair
    wide = 2 if nc % 2 == 0 else 1
    order = [list(range(i, i + wide)) for i in range(0, nc, wide)]
    few = steps <= FEW

    def cached(make):
        held = {}

        def get(step):
            if not few:
                return make(step)
            if step not in held:
                held[step] = make(step)
            return held[step]

        return get

    def total(body):
        out = jnp.zeros((rhs, wide * lanes), jnp.float32)
        if few:
            for step in range(steps):
                out = body(step, out)
            return out
        return lax.fori_loop(0, steps, body, out)

    def apply(v, high, low):
        both = jnp.dot(v, high, preferred_element_type=jnp.float32)
        return both[:rhs] + both[rhs:] + jnp.dot(v, low, preferred_element_type=jnp.float32)[:rhs]

    def hand_out(columns, partial, ref, group):
        for i, k in enumerate(columns):
            ref[nc + k] = partial[:, i * lanes : (i + 1) * lanes]
            if k:
                group.start(k, k + 1)

    def across(read):
        return lambda step: jnp.concatenate([read(step * pair + k) for k in range(pair)], axis=1)

    z_of = across(lambda k: zplane[k])
    t_of = across(lambda k: tplane[k])
    left = cached(lambda step: factors(z_of(step), True).T.astype(jnp.bfloat16))
    first_v = cached(lambda step: two(t_of(step)))

    z_plane.arrived()

    def low_part(tile):
        return (tile - tile.astype(jnp.bfloat16).astype(jnp.float32)).astype(jnp.bfloat16)

    def make_tile(i, right, step):
        tile = jnp.exp2(jnp.dot(left(step), right, preferred_element_type=jnp.float32))
        high = tile.astype(jnp.bfloat16)
        khi[i, step] = high
        if few:
            held[i, step] = tile
        else:
            klo[i, step] = low_part(tile)
        return high

    def first(i, step, out, high):
        both = jnp.dot(first_v(step), high, preferred_element_type=jnp.float32)
        return out + both[:rhs] + both[rhs:]

    for i, columns in enumerate(order):
        for k in columns:
            if k:
                source = col_of(k)
                pl.when((source > c) | (c == top))(lambda source=source: landed(source))
        right = factors(jnp.concatenate([line[col_of(k), 0:feats, :] for k in columns], axis=1), False).astype(jnp.bfloat16)
        if few and i == 0:
            for step in range(steps):
                make_tile(i, right, step)
            t_plane.arrived()
            partial = total(lambda step, out: first(i, step, out, khi[i, step]))
        else:
            if i == 0:
                t_plane.arrived()
            partial = total(lambda step, out: first(i, step, out, make_tile(i, right, step)))
        hand_out(columns, partial, part, give)
    target = tplane[0]
    along, squared = jnp.zeros((rhs, lanes), jnp.float32), jnp.zeros((rhs, lanes), jnp.float32)
    for k in range(nc):
        along = along + line[col_of(k), feats : feats + rhs, :] * part[nc + k]
        squared = squared + part[nc + k] * part[nc + k]
    early[0] = lane_sums([along, squared, target * target])
    scalars.start()
    if few:
        for i in range(len(order)):
            for step in range(steps):
                klo[i, step] = low_part(held[i, step])

    noise = column(noise_ref, rhs, lanes)
    image = part[nc] + noise * target
    give.arrived()
    for k in range(1, nc):
        image = image + part[k]

    wplane[0] = image
    wline[0] = image
    w_plane.start()
    w_line.start()
    scalars.arrived()
    sums = to_column(jnp.sum(early[...], axis=0))
    tkt, spread, tt = sums[:rhs], sums[rhs : 2 * rhs], sums[2 * rhs : 3 * rhs]
    tw = tkt + noise * tt
    alpha = tt / tw
    guess = alpha * alpha * (nc * spread + 2.0 * noise * tkt + noise * noise * tt) / tt - 1.0

    w_plane.arrived()

    def direct(t, w):
        return (t - alpha * w) + guess * t

    d_of = across(lambda k: direct(tplane[k], wplane[k]))
    second_v = cached(lambda step: two(d_of(step)))
    residual = target - alpha * image
    direction = direct(target, image)
    curved = noise * direction * direction
    for i, columns in reversed(list(enumerate(order))):
        partial = total(lambda step, out: out + apply(second_v(step), khi[i, step], klo[i, step]))
        hand_out(columns, partial, part2, give2)
        if i == len(order) - 1:
            w_line.arrived()
        for k in columns:
            curved = curved + direct(line[col_of(k), feats : feats + rhs, :], wline[k]) * part2[nc + k]
    tiny[0] = lane_sums([curved, residual * residual, direction * image])
    scalars2.start()
    base_ref[...] = alpha * target
    kept_ref[...] = residual
    image2 = part2[nc] + noise * direction
    give2.arrived()
    for k in range(1, nc):
        image2 = image2 + part2[k]
    scalars2.arrived()
    sums = to_column(jnp.sum(tiny[...], axis=0))
    curvature, norm, mixed = sums[:rhs], sums[rhs : 2 * rhs], sums[2 * rhs : 3 * rhs]
    missed = norm / tt - guess
    step_ref[...] = norm / (curvature + 2.0 * missed * mixed + missed * missed * tw)
    along_ref[...] = direction + missed * target
    image_ref[...] = image2 + missed * image
    for g in (z_plane, t_plane, give, w_line, w_plane, scalars, give2, scalars2):
        g.sent()
    pl.when(c < top)(lambda: hop(c, c + 1, 0).wait_send())
    for d in range(1, nc):
        pl.when((c >= d) & (c < top))(lambda d=d: hop(c - d, c + 1, d).wait_send())
        pl.when(c >= d)(lambda d=d: hop(c, c - d, nc + d).wait_send())


def solution(mesh):
    nr, nc = mesh.shape["row"], mesh.shape["col"]

    def on_device(points, inverse_scale, targets, noise_var):
        feats, lanes = points.shape
        rhs = targets.shape[0]
        pair = 2 if nr % 2 == 0 else 1
        wide = 2 if nc % 2 == 0 else 1
        every = nr * nc
        f32 = jnp.float32
        dma = pltpu.SemaphoreType.DMA
        tiles = (nc // wide, nr // pair, pair * lanes, wide * lanes)
        anywhere = pl.BlockSpec(memory_space=pl.ANY)
        base, step, along, kept, image = pl.pallas_call(
            functools.partial(kernel, nr, nc, feats, rhs, lanes),
            out_shape=(pltpu.VMEM((rhs, lanes), f32),) * 5,
            in_specs=[anywhere] * 4,
            out_specs=(pl.BlockSpec(memory_space=pltpu.VMEM),) * 5,
            scratch_shapes=[
                pltpu.VMEM((feats, lanes), f32),
                pltpu.SMEM((feats,), f32),
                pltpu.SMEM((rhs,), f32),
                pltpu.VMEM((nr, feats, lanes), f32),
                pltpu.VMEM((nr, rhs, lanes), f32),
                pltpu.VMEM((nc, feats + rhs, lanes), f32),
                pltpu.VMEM((2 * nc, rhs, lanes), f32),
                pltpu.VMEM((nr, rhs, lanes), f32),
                pltpu.VMEM((nc, rhs, lanes), f32),
                pltpu.VMEM((2 * nc, rhs, lanes), f32),
                pltpu.VMEM((every, 1, lanes), f32),
                pltpu.VMEM((every, 1, lanes), f32),
                pltpu.VMEM(tiles, jnp.bfloat16),
                pltpu.VMEM(tiles, jnp.bfloat16),
                pltpu.VMEM(tiles if nr // pair <= FEW else (8, 128), f32),
                dma((5,)),
                dma((10,)),
                dma((10,)),
                dma((nc,)),
                dma((2 * nc,)),
            ],
            compiler_params=pltpu.CompilerParams(
                collective_id=0, has_side_effects=True, vmem_limit_bytes=56 * 1024 * 1024
            ),
        )(points, inverse_scale, targets, noise_var)
        return base + step * along, kept - step * image

    spec = P(None, ("row", "col"))
    return jax.shard_map(
        on_device, mesh=mesh, in_specs=(spec, P(), spec, P()), out_specs=(spec, spec), check_vma=False
    )
```

```python
import functools
import math
import jax
import jax.numpy as jnp
from jax import lax
from jax.experimental import pallas as pl
from jax.experimental.pallas import tpu as pltpu
from jax.sharding import PartitionSpec as P

FEW = 8
MESH = pl.DeviceIdType.MESH
ROOT = math.sqrt(1.0 / math.log(2.0))


def loop(low, high, body, key=None):
    if high - low <= 32:
        for k in sorted(range(low, high), key=key or (lambda k: -k)):
            body(k)
    else:

        def step(k, carry):
            body(k)
            return carry

        lax.fori_loop(low, high, step, 0)


def three(x):
    high = x.astype(jnp.bfloat16).astype(jnp.float32)
    rest = x - high
    middle = rest.astype(jnp.bfloat16).astype(jnp.float32)
    return high, middle, rest - middle


def two(x):
    high = x.astype(jnp.bfloat16)
    low = (x - high.astype(jnp.float32)).astype(jnp.bfloat16)
    return jnp.concatenate([high, low], axis=0)


def factors(z, left):
    z = z * ROOT
    half = 0.5 * jnp.sum(z * z, axis=0, keepdims=True)
    h, m, l = three(z)
    a, b, c = three(-half)
    row = lax.broadcasted_iota(jnp.int32, z.shape, 0)
    norms = jnp.where(row == 0, a, jnp.where(row == 1, b, jnp.where(row == 2, c, 0.0)))
    ones = jnp.ones_like(z)
    parts = [h, h, m, h, l, m, norms, ones] if left else [h, m, h, l, h, m, ones, norms]
    return jnp.concatenate(parts, axis=0)


def column(ref, count, lanes):
    row = lax.broadcasted_iota(jnp.int32, (count, lanes), 0)
    out = jnp.zeros((count, lanes), jnp.float32)
    for k in range(count):
        out = jnp.where(row == k, ref[k], out)
    return out


def lane_sums(parts):
    used = sum(p.shape[0] for p in parts)
    parts = parts + [jnp.zeros((128 - used, 128), jnp.float32)]
    return jnp.sum(jnp.concatenate(parts, axis=0).T, axis=0, keepdims=True)


def to_column(row):
    return jnp.broadcast_to(row, (128, 128)).T


def kernel(
    nr, nc, feats, rhs, lanes,
    points_ref, scale_in, targets_ref, noise_in,
    base_ref, step_ref, along_ref, kept_ref, image_ref,
    raw, scale_ref, noise_ref, zplane, zline, tplane, tline, part, wplane, wline, part2, early, tiny, khi, klo, held,
    load_sem, send_sem, recv_sem, line_sem,
):
    r, c = lax.axis_index("row"), lax.axis_index("col")
    every = nr * nc

    def partner(position, k, count):
        if isinstance(k, int) and count & (count - 1) == 0:
            other, bit = position, 1
            while bit < count:
                if k & bit:
                    other = other + bit * (1 - 2 * lax.rem(lax.div(position, bit), 2))
                bit *= 2
            return other
        moved = position + k
        return jnp.where(moved >= count, moved - count, moved)

    rows = [partner(r, k, nr) for k in range(nr)] if every <= 32 else None
    cols = [partner(c, k, nc) for k in range(nc)] if every <= 32 else None

    def at(kr, kc):
        if rows is not None:
            return (rows[kr], cols[kc])
        return (partner(r, kr, nr), partner(c, kc, nc))

    def distance(k):
        kr, kc = k // nc, k % nc
        return kc + bin(kr // 2).count("1") + 0.5 * (kr % 2)

    barrier = pltpu.get_barrier_semaphore()
    loop(1, nc, lambda k: pl.semaphore_signal(barrier, inc=1, device_id=at(0, k), device_id_type=MESH))
    loop(1, nr, lambda k: pl.semaphore_signal(barrier, inc=1, device_id=at(k, 0), device_id_type=MESH))
    loads = [
        pltpu.make_async_copy(src, dst, load_sem.at[i])
        for i, (src, dst) in enumerate([
            (points_ref, raw), (scale_in, scale_ref), (targets_ref, tplane.at[0]),
            (targets_ref, tline.at[0]), (noise_in, noise_ref),
        ])
    ]
    for load in loads:
        load.start()
    loads[0].wait()
    loads[1].wait()
    scaled = raw[...] * column(scale_ref, feats, lanes)
    zplane[0] = scaled
    zline[0] = scaled
    for load in loads[2:]:
        load.wait()
    pl.semaphore_wait(barrier, nr + nc - 2)

    class Group:
        count = 0

        def __init__(self, ref, last, peer, src=lambda k: 0, slot_sems=None, key=None):
            self.ref, self.last, self.peer, self.src = ref, last, peer, src
            self.slot_sems, self.key = slot_sems, key
            self.sem = Group.count
            Group.count += 1

        def start(self, low=1, high=None):
            def one(k):
                arrival = recv_sem.at[self.sem] if self.slot_sems is None else self.slot_sems.at[k]
                pltpu.make_async_remote_copy(
                    src_ref=self.ref.at[self.src(k)], dst_ref=self.ref.at[k],
                    send_sem=send_sem.at[self.sem], recv_sem=arrival,
                    device_id=self.peer(k), device_id_type=MESH,
                ).start()

            loop(low, self.last if high is None else high, one, self.key)

        def wait(self, sem):
            slots = self.ref.at[pl.ds(1, self.last - 1)]
            pltpu.make_async_copy(slots, slots, sem.at[self.sem]).wait()

        def wait_slot(self, k):
            pltpu.make_async_copy(self.ref.at[k], self.ref.at[k], self.slot_sems.at[k]).wait()

        def arrived(self):
            self.wait(recv_sem)

        def sent(self):
            self.wait(send_sem)

    along_col = lambda k: at(0, k)
    along_row = lambda k: at(k, 0)
    back_col = lambda k: at(0, k if nc & (nc - 1) == 0 else nc - k)
    anywhere = lambda k: at(k // nc, k % nc)
    z_line = Group(zline, nc, along_col, slot_sems=line_sem)
    z_plane = Group(zplane, nr, along_row)
    t_line = Group(tline, nc, along_col)
    t_plane = Group(tplane, nr, along_row)
    give = Group(part, nc, back_col, lambda k: nc + k)
    w_line = Group(wline, nc, along_col)
    w_plane = Group(wplane, nr, along_row)
    scalars = Group(early, every, anywhere, key=lambda k: -distance(k))
    give2 = Group(part2, nc, back_col, lambda k: nc + k)
    scalars2 = Group(tiny, every, anywhere, key=lambda k: -distance(k))

    z_line.start()
    z_plane.start()
    t_plane.start()
    t_line.start()

    pair = 2 if nr % 2 == 0 else 1
    steps = nr // pair
    wide = math.gcd(nc, 4)
    order = [list(range(i, i + wide)) for i in range(0, nc, wide)]
    few = steps <= FEW

    def cached(make):
        held = {}

        def get(step):
            if not few:
                return make(step)
            if step not in held:
                held[step] = make(step)
            return held[step]

        return get

    def total(body):
        out = jnp.zeros((rhs, wide * lanes), jnp.float32)
        if few:
            for step in range(steps):
                out = body(step, out)
            return out
        return lax.fori_loop(0, steps, body, out)

    def apply(v, high, low):
        both = jnp.dot(v, high, preferred_element_type=jnp.float32)
        return both[:rhs] + both[rhs:] + jnp.dot(v, low, preferred_element_type=jnp.float32)[:rhs]

    def hand_out(columns, partial, ref, group):
        for i, k in enumerate(columns):
            ref[nc + k] = partial[:, i * lanes : (i + 1) * lanes]
            if k:
                group.start(k, k + 1)

    def across(read):
        return lambda step: jnp.concatenate([read(step * pair + k) for k in range(pair)], axis=1)

    z_of = across(lambda k: zplane[k])
    t_of = across(lambda k: tplane[k])
    left = cached(lambda step: factors(z_of(step), True).T.astype(jnp.bfloat16))
    first_v = cached(lambda step: two(t_of(step)))

    z_plane.arrived()

    def low_part(tile):
        return (tile - tile.astype(jnp.bfloat16).astype(jnp.float32)).astype(jnp.bfloat16)

    def make_tile(i, right, step):
        tile = jnp.exp2(jnp.dot(left(step), right, preferred_element_type=jnp.float32))
        high = tile.astype(jnp.bfloat16)
        khi[i, step] = high
        if few:
            held[i, step] = tile
        else:
            klo[i, step] = low_part(tile)
        return high

    def first(i, step, out, high):
        both = jnp.dot(first_v(step), high, preferred_element_type=jnp.float32)
        return out + both[:rhs] + both[rhs:]

    for i, columns in enumerate(order):
        for k in columns:
            if k:
                z_line.wait_slot(k)
        right = factors(jnp.concatenate([zline[k] for k in columns], axis=1), False).astype(jnp.bfloat16)
        if few and i == 0:
            for step in range(steps):
                make_tile(i, right, step)
            t_plane.arrived()
            partial = total(lambda step, out: first(i, step, out, khi[i, step]))
        else:
            if i == 0:
                t_plane.arrived()
            partial = total(lambda step, out: first(i, step, out, make_tile(i, right, step)))
        hand_out(columns, partial, part, give)
    target = tplane[0]
    t_line.arrived()
    along, squared = jnp.zeros((rhs, lanes), jnp.float32), jnp.zeros((rhs, lanes), jnp.float32)
    for k in range(nc):
        along = along + tline[k] * part[nc + k]
        squared = squared + part[nc + k] * part[nc + k]
    early[0] = lane_sums([along, squared, target * target])
    scalars.start()
    if few:
        for i in range(len(order)):
            for step in range(steps):
                klo[i, step] = low_part(held[i, step])

    noise = column(noise_ref, rhs, lanes)
    image = part[nc] + noise * target
    give.arrived()
    for k in range(1, nc):
        image = image + part[k]

    wplane[0] = image
    wline[0] = image
    w_plane.start()
    w_line.start()
    scalars.arrived()
    sums = to_column(jnp.sum(early[...], axis=0))
    tkt, spread, tt = sums[:rhs], sums[rhs : 2 * rhs], sums[2 * rhs : 3 * rhs]
    tw = tkt + noise * tt
    alpha = tt / tw
    guess = alpha * alpha * (nc * spread + 2.0 * noise * tkt + noise * noise * tt) / tt - 1.0

    w_plane.arrived()

    def direct(t, w):
        return (t - alpha * w) + guess * t

    d_of = across(lambda k: direct(tplane[k], wplane[k]))
    second_v = cached(lambda step: two(d_of(step)))
    residual = target - alpha * image
    direction = direct(target, image)
    curved = noise * direction * direction
    for i, columns in reversed(list(enumerate(order))):
        partial = total(lambda step, out: out + apply(second_v(step), khi[i, step], klo[i, step]))
        hand_out(columns, partial, part2, give2)
        if i == len(order) - 1:
            w_line.arrived()
        for k in columns:
            curved = curved + direct(tline[k], wline[k]) * part2[nc + k]
    tiny[0] = lane_sums([curved, residual * residual, direction * image])
    scalars2.start()
    base_ref[...] = alpha * target
    kept_ref[...] = residual
    image2 = part2[nc] + noise * direction
    give2.arrived()
    for k in range(1, nc):
        image2 = image2 + part2[k]
    scalars2.arrived()
    sums = to_column(jnp.sum(tiny[...], axis=0))
    curvature, norm, mixed = sums[:rhs], sums[rhs : 2 * rhs], sums[2 * rhs : 3 * rhs]
    missed = norm / tt - guess
    step_ref[...] = norm / (curvature + 2.0 * missed * mixed + missed * missed * tw)
    along_ref[...] = direction + missed * target
    image_ref[...] = image2 + missed * image
    for g in (z_line, z_plane, t_plane, t_line, give, w_line, w_plane, scalars, give2, scalars2):
        g.sent()


def solution(mesh):
    nr, nc = mesh.shape["row"], mesh.shape["col"]

    def on_device(points, inverse_scale, targets, noise_var):
        feats, lanes = points.shape
        rhs = targets.shape[0]
        pair = 2 if nr % 2 == 0 else 1
        wide = math.gcd(nc, 4)
        every = nr * nc
        f32 = jnp.float32
        dma = pltpu.SemaphoreType.DMA
        tiles = (nc // wide, nr // pair, pair * lanes, wide * lanes)
        anywhere = pl.BlockSpec(memory_space=pl.ANY)
        base, step, along, kept, image = pl.pallas_call(
            functools.partial(kernel, nr, nc, feats, rhs, lanes),
            out_shape=(pltpu.VMEM((rhs, lanes), f32),) * 5,
            in_specs=[anywhere] * 4,
            out_specs=(pl.BlockSpec(memory_space=pltpu.VMEM),) * 5,
            scratch_shapes=[
                pltpu.VMEM((feats, lanes), f32),
                pltpu.SMEM((feats,), f32),
                pltpu.SMEM((rhs,), f32),
                pltpu.VMEM((nr, feats, lanes), f32),
                pltpu.VMEM((nc, feats, lanes), f32),
                pltpu.VMEM((nr, rhs, lanes), f32),
                pltpu.VMEM((nc, rhs, lanes), f32),
                pltpu.VMEM((2 * nc, rhs, lanes), f32),
                pltpu.VMEM((nr, rhs, lanes), f32),
                pltpu.VMEM((nc, rhs, lanes), f32),
                pltpu.VMEM((2 * nc, rhs, lanes), f32),
                pltpu.VMEM((every, 1, lanes), f32),
                pltpu.VMEM((every, 1, lanes), f32),
                pltpu.VMEM(tiles, jnp.bfloat16),
                pltpu.VMEM(tiles, jnp.bfloat16),
                pltpu.VMEM(tiles if nr // pair <= FEW else (8, 128), f32),
                dma((5,)),
                dma((10,)),
                dma((10,)),
                dma((nc,)),
            ],
            compiler_params=pltpu.CompilerParams(
                collective_id=0, has_side_effects=True, vmem_limit_bytes=56 * 1024 * 1024
            ),
        )(points, inverse_scale, targets, noise_var)
        return base + step * along, kept - step * image

    spec = P(None, ("row", "col"))
    return jax.shard_map(
        on_device, mesh=mesh, in_specs=(spec, P(), spec, P()), out_specs=(spec, spec), check_vma=False
    )
```

```python
import functools
import math
import jax
import jax.numpy as jnp
from jax import lax
from jax.experimental import pallas as pl
from jax.experimental.pallas import tpu as pltpu
from jax.sharding import PartitionSpec as P

FEW = 8
MESH = pl.DeviceIdType.MESH
ROOT = math.sqrt(1.0 / math.log(2.0))


def loop(low, high, body, key=None):
    if high - low <= 32:
        for k in sorted(range(low, high), key=key or (lambda k: -k)):
            body(k)
    else:

        def step(k, carry):
            body(k)
            return carry

        lax.fori_loop(low, high, step, 0)


def three(x):
    high = x.astype(jnp.bfloat16).astype(jnp.float32)
    rest = x - high
    middle = rest.astype(jnp.bfloat16).astype(jnp.float32)
    return high, middle, rest - middle


def two(x):
    high = x.astype(jnp.bfloat16)
    low = (x - high.astype(jnp.float32)).astype(jnp.bfloat16)
    return jnp.concatenate([high, low], axis=0)


def factors(z, left):
    z = z * ROOT
    half = 0.5 * jnp.sum(z * z, axis=0, keepdims=True)
    h, m, l = three(z)
    a, b, c = three(-half)
    row = lax.broadcasted_iota(jnp.int32, z.shape, 0)
    norms = jnp.where(row == 0, a, jnp.where(row == 1, b, jnp.where(row == 2, c, 0.0)))
    ones = jnp.ones_like(z)
    parts = [h, h, m, h, l, m, norms, ones] if left else [h, m, h, l, h, m, ones, norms]
    return jnp.concatenate(parts, axis=0)


def column(ref, count, lanes):
    row = lax.broadcasted_iota(jnp.int32, (count, lanes), 0)
    out = jnp.zeros((count, lanes), jnp.float32)
    for k in range(count):
        out = jnp.where(row == k, ref[k], out)
    return out


def lane_sums(parts):
    used = sum(p.shape[0] for p in parts)
    parts = parts + [jnp.zeros((128 - used, 128), jnp.float32)]
    return jnp.sum(jnp.concatenate(parts, axis=0).T, axis=0, keepdims=True)


def to_column(row):
    return jnp.broadcast_to(row, (128, 128)).T


def kernel(
    nr, nc, feats, rhs, lanes,
    points_ref, scale_in, targets_ref, noise_in,
    base_ref, step_ref, along_ref, kept_ref, image_ref,
    raw, scale_ref, noise_ref, zplane, zline, tplane, tline, part, wplane, wline, part2, early, tiny, khi, klo, held,
    load_sem, send_sem, recv_sem, line_sem,
):
    r, c = lax.axis_index("row"), lax.axis_index("col")
    every = nr * nc

    def partner(position, k, count):
        if isinstance(k, int) and count & (count - 1) == 0:
            other, bit = position, 1
            while bit < count:
                if k & bit:
                    other = other + bit * (1 - 2 * lax.rem(lax.div(position, bit), 2))
                bit *= 2
            return other
        moved = position + k
        return jnp.where(moved >= count, moved - count, moved)

    rows = [partner(r, k, nr) for k in range(nr)] if every <= 32 else None
    cols = [partner(c, k, nc) for k in range(nc)] if every <= 32 else None

    def at(kr, kc):
        if rows is not None:
            return (rows[kr], cols[kc])
        return (partner(r, kr, nr), partner(c, kc, nc))

    def distance(k):
        kr, kc = k // nc, k % nc
        return kc + bin(kr // 2).count("1") + 0.5 * (kr % 2)

    barrier = pltpu.get_barrier_semaphore()
    loop(1, nc, lambda k: pl.semaphore_signal(barrier, inc=1, device_id=at(0, k), device_id_type=MESH))
    loop(1, nr, lambda k: pl.semaphore_signal(barrier, inc=1, device_id=at(k, 0), device_id_type=MESH))
    loads = [
        pltpu.make_async_copy(src, dst, load_sem.at[i])
        for i, (src, dst) in enumerate([
            (points_ref, raw), (scale_in, scale_ref), (targets_ref, tplane.at[0]),
            (targets_ref, tline.at[0]), (noise_in, noise_ref),
        ])
    ]
    for load in loads:
        load.start()
    loads[0].wait()
    loads[1].wait()
    scaled = raw[...] * column(scale_ref, feats, lanes)
    zplane[0] = scaled
    zline[0] = scaled
    for load in loads[2:]:
        load.wait()
    pl.semaphore_wait(barrier, nr + nc - 2)

    class Group:
        count = 0

        def __init__(self, ref, last, peer, src=lambda k: 0, slot_sems=None, key=None):
            self.ref, self.last, self.peer, self.src = ref, last, peer, src
            self.slot_sems, self.key = slot_sems, key
            self.sem = Group.count
            Group.count += 1

        def start(self, low=1, high=None):
            def one(k):
                arrival = recv_sem.at[self.sem] if self.slot_sems is None else self.slot_sems.at[k]
                pltpu.make_async_remote_copy(
                    src_ref=self.ref.at[self.src(k)], dst_ref=self.ref.at[k],
                    send_sem=send_sem.at[self.sem], recv_sem=arrival,
                    device_id=self.peer(k), device_id_type=MESH,
                ).start()

            loop(low, self.last if high is None else high, one, self.key)

        def wait(self, sem):
            slots = self.ref.at[pl.ds(1, self.last - 1)]
            pltpu.make_async_copy(slots, slots, sem.at[self.sem]).wait()

        def wait_slot(self, k):
            pltpu.make_async_copy(self.ref.at[k], self.ref.at[k], self.slot_sems.at[k]).wait()

        def arrived(self):
            self.wait(recv_sem)

        def sent(self):
            self.wait(send_sem)

    along_col = lambda k: at(0, k)
    along_row = lambda k: at(k, 0)
    back_col = lambda k: at(0, k if nc & (nc - 1) == 0 else nc - k)
    anywhere = lambda k: at(k // nc, k % nc)
    z_line = Group(zline, nc, along_col, slot_sems=line_sem)
    z_plane = Group(zplane, nr, along_row)
    t_line = Group(tline, nc, along_col)
    t_plane = Group(tplane, nr, along_row)
    give = Group(part, nc, back_col, lambda k: nc + k)
    w_line = Group(wline, nc, along_col)
    w_plane = Group(wplane, nr, along_row)
    scalars = Group(early, every, anywhere, key=lambda k: -distance(k))
    give2 = Group(part2, nc, back_col, lambda k: nc + k)
    scalars2 = Group(tiny, every, anywhere, key=lambda k: -distance(k))

    z_line.start()
    z_plane.start()
    t_plane.start()
    t_line.start()

    pair = 2 if nr % 2 == 0 else 1
    steps = nr // pair
    wide = math.gcd(nc, 4)
    order = [list(range(i, i + wide)) for i in range(0, nc, wide)]
    few = steps <= FEW

    def cached(make):
        held = {}

        def get(step):
            if not few:
                return make(step)
            if step not in held:
                held[step] = make(step)
            return held[step]

        return get

    def total(body):
        out = jnp.zeros((rhs, wide * lanes), jnp.float32)
        if few:
            for step in range(steps):
                out = body(step, out)
            return out
        return lax.fori_loop(0, steps, body, out)

    def apply(v, high, low):
        both = jnp.dot(v, high, preferred_element_type=jnp.float32)
        return both[:rhs] + both[rhs:] + jnp.dot(v, low, preferred_element_type=jnp.float32)[:rhs]

    def hand_out(columns, partial, ref, group):
        for i, k in enumerate(columns):
            ref[nc + k] = partial[:, i * lanes : (i + 1) * lanes]
            if k:
                group.start(k, k + 1)

    def across(read):
        return lambda step: jnp.concatenate([read(step * pair + k) for k in range(pair)], axis=1)

    z_of = across(lambda k: zplane[k])
    t_of = across(lambda k: tplane[k])
    left = cached(lambda step: factors(z_of(step), True).T.astype(jnp.bfloat16))
    first_v = cached(lambda step: two(t_of(step)))

    z_plane.arrived()

    def low_part(tile):
        return (tile - tile.astype(jnp.bfloat16).astype(jnp.float32)).astype(jnp.bfloat16)

    def make_tile(i, right, step):
        tile = jnp.exp2(jnp.dot(left(step), right, preferred_element_type=jnp.float32))
        high = tile.astype(jnp.bfloat16)
        khi[i, step] = high
        if few:
            held[i, step] = tile
        else:
            klo[i, step] = low_part(tile)
        return high

    def first(i, step, out, high):
        both = jnp.dot(first_v(step), high, preferred_element_type=jnp.float32)
        return out + both[:rhs] + both[rhs:]

    for i, columns in enumerate(order):
        for k in columns:
            if k:
                z_line.wait_slot(k)
        right = factors(jnp.concatenate([zline[k] for k in columns], axis=1), False).astype(jnp.bfloat16)
        if few and i == 0:
            for step in range(steps):
                make_tile(i, right, step)
            t_plane.arrived()
            partial = total(lambda step, out: first(i, step, out, khi[i, step]))
        else:
            if i == 0:
                t_plane.arrived()
            partial = total(lambda step, out: first(i, step, out, make_tile(i, right, step)))
        hand_out(columns, partial, part, give)
    target = tplane[0]
    t_line.arrived()
    along, squared = jnp.zeros((rhs, lanes), jnp.float32), jnp.zeros((rhs, lanes), jnp.float32)
    for k in range(nc):
        along = along + tline[k] * part[nc + k]
        squared = squared + part[nc + k] * part[nc + k]
    early[0] = lane_sums([along, squared, target * target])
    scalars.start()

    noise = column(noise_ref, rhs, lanes)
    image = part[nc] + noise * target
    give.arrived()
    for k in range(1, nc):
        image = image + part[k]

    wplane[0] = image
    wline[0] = image
    w_plane.start()
    w_line.start()
    if few:
        for i in range(len(order)):
            for step in range(steps):
                klo[i, step] = low_part(held[i, step])
    scalars.arrived()
    sums = to_column(jnp.sum(early[...], axis=0))
    tkt, spread, tt = sums[:rhs], sums[rhs : 2 * rhs], sums[2 * rhs : 3 * rhs]
    tw = tkt + noise * tt
    alpha = tt / tw
    guess = alpha * alpha * (nc * spread + 2.0 * noise * tkt + noise * noise * tt) / tt - 1.0

    w_plane.arrived()

    def direct(t, w):
        return (t - alpha * w) + guess * t

    d_of = across(lambda k: direct(tplane[k], wplane[k]))
    second_v = cached(lambda step: two(d_of(step)))
    residual = target - alpha * image
    direction = direct(target, image)
    curved = noise * direction * direction
    for i, columns in reversed(list(enumerate(order))):
        partial = total(lambda step, out: out + apply(second_v(step), khi[i, step], klo[i, step]))
        hand_out(columns, partial, part2, give2)
        if i == len(order) - 1:
            w_line.arrived()
        for k in columns:
            curved = curved + direct(tline[k], wline[k]) * part2[nc + k]
    tiny[0] = lane_sums([curved, residual * residual, direction * image])
    scalars2.start()
    base_ref[...] = alpha * target
    kept_ref[...] = residual
    image2 = part2[nc] + noise * direction
    give2.arrived()
    for k in range(1, nc):
        image2 = image2 + part2[k]
    scalars2.arrived()
    sums = to_column(jnp.sum(tiny[...], axis=0))
    curvature, norm, mixed = sums[:rhs], sums[rhs : 2 * rhs], sums[2 * rhs : 3 * rhs]
    missed = norm / tt - guess
    step_ref[...] = norm / (curvature + 2.0 * missed * mixed + missed * missed * tw)
    along_ref[...] = direction + missed * target
    image_ref[...] = image2 + missed * image
    for g in (z_line, z_plane, t_plane, t_line, give, w_line, w_plane, scalars, give2, scalars2):
        g.sent()


def solution(mesh):
    nr, nc = mesh.shape["row"], mesh.shape["col"]

    def on_device(points, inverse_scale, targets, noise_var):
        feats, lanes = points.shape
        rhs = targets.shape[0]
        pair = 2 if nr % 2 == 0 else 1
        wide = math.gcd(nc, 4)
        every = nr * nc
        f32 = jnp.float32
        dma = pltpu.SemaphoreType.DMA
        tiles = (nc // wide, nr // pair, pair * lanes, wide * lanes)
        anywhere = pl.BlockSpec(memory_space=pl.ANY)
        base, step, along, kept, image = pl.pallas_call(
            functools.partial(kernel, nr, nc, feats, rhs, lanes),
            out_shape=(pltpu.VMEM((rhs, lanes), f32),) * 5,
            in_specs=[anywhere] * 4,
            out_specs=(pl.BlockSpec(memory_space=pltpu.VMEM),) * 5,
            scratch_shapes=[
                pltpu.VMEM((feats, lanes), f32),
                pltpu.SMEM((feats,), f32),
                pltpu.SMEM((rhs,), f32),
                pltpu.VMEM((nr, feats, lanes), f32),
                pltpu.VMEM((nc, feats, lanes), f32),
                pltpu.VMEM((nr, rhs, lanes), f32),
                pltpu.VMEM((nc, rhs, lanes), f32),
                pltpu.VMEM((2 * nc, rhs, lanes), f32),
                pltpu.VMEM((nr, rhs, lanes), f32),
                pltpu.VMEM((nc, rhs, lanes), f32),
                pltpu.VMEM((2 * nc, rhs, lanes), f32),
                pltpu.VMEM((every, 1, lanes), f32),
                pltpu.VMEM((every, 1, lanes), f32),
                pltpu.VMEM(tiles, jnp.bfloat16),
                pltpu.VMEM(tiles, jnp.bfloat16),
                pltpu.VMEM(tiles if nr // pair <= FEW else (8, 128), f32),
                dma((5,)),
                dma((10,)),
                dma((10,)),
                dma((nc,)),
            ],
            compiler_params=pltpu.CompilerParams(
                collective_id=0, has_side_effects=True, vmem_limit_bytes=56 * 1024 * 1024
            ),
        )(points, inverse_scale, targets, noise_var)
        return base + step * along, kept - step * image

    spec = P(None, ("row", "col"))
    return jax.shard_map(
        on_device, mesh=mesh, in_specs=(spec, P(), spec, P()), out_specs=(spec, spec), check_vma=False
    )
```
